32 devices in a mesh: grp: 2 (over x), wave: 16 (over z, y, core).
Axes of the slice: x: 2, y: 2, z: 4, core: 2. Of those that a mesh axis runs over, the one named last changes fastest.
Arguments:
- spectral: bfloat16 [640, 641, 256], P(('grp', 'wave')), parts along dimension 0, may hold values from -0.23925781 to 0.23925781
- legendre: bfloat16 [320, 641, 320], P('wave'), may hold values from -0.25 to 0.25
- pair_low: int32 [320], replicated, may hold values from 0 to 319, each once
- routes: int32 [102400, 1], P(('grp', 'wave')), parts along dimension 0, may hold values from 0 to 15; in each aligned block of 3200 rows (0 to 3199, 3200 to 6399, ...) at most 400 rows name the same one
- w_in: bfloat16 [16, 128, 1024], P('wave'), may hold values from -0.5 to 0.5
- w_mid: bfloat16 [16, 1024, 1024], P('wave'), may hold values from -0.1875 to 0.1875
- w_out: bfloat16 [16, 1024, 128], P('wave'), may hold values from -1.5 to 1.5
Outputs:
- tendency: bfloat16 [640, 641, 256], P(('grp', 'wave')), parts along dimension 0
The draws below stay inside these ranges and needn't reach their ends.
There are 2 independent parts, one for each index of `grp`. The reference program is written for one: setup_inputs(seed, part) draws one part's arguments, and reference() takes and returns one part's arrays. A program takes and returns all parts, laid end to end along the dimension named above; an argument that names none is the same for every part. Nothing has to cross between parts.
Inputs may be any that keep to these rules, and one draw needn't show every extreme that they name: `routes`: among the columns of one device (each aligned block of 3200 columns) at most 400 name the same network, a bound that some block reaches of them.
All inputs are finite; a program needn't handle non-finite values.
Results may differ from the reference program's by a relative error of at most 0.01.
Values may be sent and summed in bfloat16 or wider, within the bound.
No kernel may reach another device: no remote copies, remote signals or barrier semaphores. Data moves between devices by JAX's collectives and lax.ppermute only.
A program may use at most 192 MiB of HBM per device.

```python
import math
import jax
import jax.numpy as jnp
import numpy as np
from jax import lax

M = 640
LAT = 320
NLON = 1280
FIELDS = 4
HID = 1024
PAIRS = 320
J = 641
FL = 128
C = 256
COLUMNS = 51200
COLS_DEV = 3200
EXPERTS = 16
CAP = 400
N_WAVE = 16


def block_levels(own_key, dims, cuts, least, top_value):
    gain, own = 1.0, jax.random.fold_in(own_key, 6)
    for axis_at, parts in cuts:
        draws = jnp.exp(jax.random.uniform(jax.random.fold_in(own, axis_at), (parts,), jnp.float32, least / len(cuts), top_value / len(cuts)))
        gain = gain * jnp.repeat(draws, dims[axis_at] // parts).reshape([-1 if axis == axis_at else 1 for axis in range(len(dims))])
    return gain


def assign_block(rng, own, number, rows, number_of, top, reach, lean):
    order = jax.random.permutation(rng, number_of)
    packed, ordinary = shares(number_of, rows * top, reach, lean, True), shares(number_of, rows * top, reach, lean, False)
    places = jnp.arange(number_of)

    def named(sizes, rotation):
        used = int((sizes > 0).sum())
        fixed = max(1, used // 4)
        passed = fixed + (places - fixed + rotation * (used - fixed)) % max(1, number_of - fixed)
        return jnp.zeros((number_of,), jnp.int32).at[order[jnp.where(places < fixed, places, passed)]].set(jnp.asarray(sizes, jnp.int32))

    sizes = jnp.where(number % 4 == 0, named(packed, number // 4), named(ordinary, number - number // 4 - 1))
    mixed = jax.random.permutation(jax.random.fold_in(own, 3), number_of)
    giver, taker = mixed[0:number_of // 2 * 2:2], mixed[1:number_of // 2 * 2:2]
    slack = jnp.minimum(sizes[giver] - 1, reach - sizes[taker]) // 2
    slack = jnp.where((giver == order[0]) | (taker == order[0]) | (sizes[taker] == 0), 0, jnp.maximum(slack, 0))
    passed = jax.random.randint(jax.random.fold_in(own, 4), (number_of // 2,), 0, 1 << 20) % (slack + 1)
    sizes = sizes.at[giver].add(-passed).at[taker].add(passed)
    items = jnp.searchsorted(jnp.cumsum(sizes), jnp.arange(rows * top), side="right").astype(jnp.int32)
    listing = items.reshape(top, rows).T
    listing = listing[jax.random.permutation(jax.random.fold_in(own, 1), rows)]
    rotation = jax.random.randint(jax.random.fold_in(own, 2), (rows, 1), 0, top)
    return jnp.take_along_axis(listing, (jnp.arange(top)[None, :] + rotation) % top, axis=1)


def shares(count, total, limit, slope, full):
    portions = [(1 << 20) // math.isqrt(grade ** slope) + 1 for grade in range(1, count + 1)]
    largest = limit if full else min(limit, max(-(-total // count), total * portions[0] // sum(portions)))
    least = 1 if total - largest >= count - 1 else 0
    counts, surplus = [largest] + [least] * (count - 1), total - largest - least * (count - 1)
    while surplus > 0:
        free = [i for i in range(1, count) if counts[i] < largest] or [i for i in range(1, count) if counts[i] < limit]
        whole, remaining = sum([portions[i] for i in free]), surplus
        for i in free:
            more = min(limit - counts[i], max(1, remaining * portions[i] // whole), surplus)
            counts[i] = counts[i] + more
            surplus = surplus - more
    return np.array(counts)


def bell_draw(rng, shape, width, limit, shards=(), held_as=jnp.bfloat16):
    entries = jax.random.normal(rng, shape, jnp.float32) * width
    if len(shards) > 0:
        entries = block_levels(rng, shape, shards, -0.22, 0.18) * entries
    return jnp.clip(entries, min=-limit, max=limit).astype(held_as)


def setup_inputs(seed: int = 0, part: int = 0) -> dict:
    keys = jax.random.split(jax.random.key(seed), 8)
    part_splits = jax.random.split(jax.random.fold_in(keys[7], part), 8)
    spectral = bell_draw(part_splits[0], (PAIRS, J, C), 0.04, 0.23925781, ((0, 16),))
    legendre = bell_draw(keys[1], (PAIRS, J, LAT), J ** -0.5, 0.25, ((0, 16),))
    pair_low = jax.random.permutation(keys[2], PAIRS).astype(jnp.int32)
    routes_keys = jax.random.split(jax.random.fold_in(part_splits[3], 1), COLUMNS // COLS_DEV)
    routes_turns = jax.random.permutation(jax.random.fold_in(part_splits[3], 3), COLUMNS // COLS_DEV)
    routes = jax.vmap(lambda own, number: assign_block(jax.random.fold_in(part_splits[3], 2), own, number, COLS_DEV, EXPERTS, 1, CAP, 2))(routes_keys, routes_turns).reshape((COLUMNS, 1))
    w_in = bell_draw(keys[4], (EXPERTS, FL, HID), FL ** -0.5, 0.5, ((0, 16),))
    w_mid = bell_draw(keys[5], (EXPERTS, HID, HID), HID ** -0.5, 0.1875, ((0, 16),))
    w_out = bell_draw(keys[6], (EXPERTS, HID, FL), 0.25, 1.5, ((0, 16),))
    return dict(spectral=spectral, legendre=legendre, pair_low=pair_low, routes=routes, w_in=w_in, w_mid=w_mid, w_out=w_out)


def slot_waves(pair_low, wave_total):
    lower_wave = pair_low.astype(jnp.int32)
    return jnp.stack([lower_wave, wave_total - 1 - lower_wave], axis=1).reshape(-1)

def side_masks(pair_low, wave_total):
    degree = jnp.arange(wave_total + 1, dtype=jnp.int32)
    lower_side = degree[None, :] < (wave_total - pair_low.astype(jnp.int32))[:, None]
    return jnp.stack([lower_side, jnp.logical_not(lower_side)], axis=1)

def fourier_table(wavenums, points, inverse):
    longitude = jnp.arange(points, dtype=jnp.int32)
    phases = wavenums[:, None] * longitude[None, :] % points
    angles = phases.astype(jnp.float32) * jnp.float32(2.0 * math.pi / points)
    if inverse:
        factor = jnp.where(wavenums == 0, jnp.float32(1.0), jnp.float32(2.0))[:, None]
    else:
        factor = jnp.full((wavenums.shape[0], 1), 1.0 / math.sqrt(points), jnp.float32)
    return jnp.stack([factor * jnp.cos(angles), -factor * jnp.sin(angles)], axis=1).astype(jnp.bfloat16)

def forcing(grid_fields):
    flattened = grid_fields.reshape(FIELDS, -1)
    return (flattened * jnp.roll(flattened, -1, axis=0)).reshape(grid_fields.shape)

def coarse_columns(grid_fields):
    feat_width = grid_fields.shape[0]
    lat_rows = grid_fields.shape[1]
    lon_count = grid_fields.shape[2]
    blocks = grid_fields.reshape(feat_width, lat_rows // 2, 2, lon_count // 4, 4).mean(axis=(2, 4))
    return blocks.reshape(feat_width, -1).T.astype(jnp.bfloat16)

def spread_back(values, lat_rows):
    feat_width = values.shape[1]
    coarse = values.astype(jnp.float32).T.reshape(feat_width, lat_rows // 2, -1)
    before = jnp.roll(coarse, 1, axis=2)
    following = jnp.roll(coarse, -1, axis=2)
    pieces = [0.375 * before + 0.625 * coarse, 0.125 * before + 0.875 * coarse, 0.875 * coarse + 0.125 * following, 0.625 * coarse + 0.375 * following]
    fine_grid = jnp.stack(pieces, axis=3).reshape(feat_width, lat_rows // 2, -1)
    return jnp.repeat(fine_grid, 2, axis=1)

def slot_positions(regimes, experts_total):
    onehot = (regimes[:, :, None] == jnp.arange(experts_total, dtype=jnp.int32)).astype(jnp.int32)
    ranking = jnp.cumsum(onehot, axis=1) - 1
    return lax.optimization_barrier(jnp.sum(ranking * onehot, axis=2))

def network(columns, weight_in, weight_mid, weight_out):
    hidden = jax.nn.silu(jnp.dot(columns, weight_in, preferred_element_type=jnp.float32)).astype(jnp.bfloat16)
    deeper = jax.nn.silu(jnp.dot(hidden, weight_mid, preferred_element_type=jnp.float32)).astype(jnp.bfloat16)
    return jnp.dot(deeper, weight_out, preferred_element_type=jnp.float32).astype(jnp.bfloat16)

def reference(spectral, legendre, pair_low, routes, w_in, w_mid, w_out):
    pair_count = spectral.shape[0]
    degrees = spectral.shape[1]
    channels = spectral.shape[2]
    feat_width = channels // 2
    side_mask = side_masks(pair_low, M)

    def inverse_pair(bundle):
        coeffs, pair_table, side_rows = bundle
        masked = jnp.where(side_rows[:, :, None], coeffs.astype(jnp.float32)[None], 0.0)
        return jnp.einsum('sjc,jl->scl', masked, pair_table.astype(jnp.float32)).astype(jnp.bfloat16)
    fourier_in = lax.map(inverse_pair, (spectral, legendre, side_mask))
    fourier_in = fourier_in.reshape(2 * pair_count, feat_width, 2, LAT)
    wavenums = slot_waves(pair_low, M)
    inverse_table = fourier_table(wavenums, NLON, True)
    grid_fields = jnp.einsum('qfra,qrl->fal', fourier_in.astype(jnp.float32), inverse_table.astype(jnp.float32))
    forced = forcing(grid_fields)
    columns = coarse_columns(grid_fields)
    regimes = routes[:, 0].astype(jnp.int32).reshape(N_WAVE, COLS_DEV)
    positions = slot_positions(regimes, EXPERTS)
    sources = jnp.broadcast_to(jnp.arange(N_WAVE, dtype=jnp.int32)[:, None], regimes.shape)
    regime_flat = regimes.reshape(-1)
    source_flat = sources.reshape(-1)
    position_flat = positions.reshape(-1)
    buffer = jnp.zeros((EXPERTS, N_WAVE, CAP, feat_width), jnp.bfloat16)
    buffer = buffer.at[regime_flat, source_flat, position_flat].set(columns)

    def run_expert(bundle):
        block_rows, weight_in, weight_mid, weight_out = bundle
        return network(block_rows.reshape(-1, feat_width), weight_in, weight_mid, weight_out).reshape(block_rows.shape)
    results = lax.map(run_expert, (buffer, w_in, w_mid, w_out))
    returned = results[regime_flat, source_flat, position_flat]
    correction = spread_back(returned, LAT)
    tendency_grid = (forced + correction).astype(jnp.bfloat16)
    forward_table = fourier_table(wavenums, NLON, False)
    fourier_out = jnp.einsum('fal,qrl->qfra', tendency_grid.astype(jnp.float32), forward_table.astype(jnp.float32)).astype(jnp.bfloat16)
    fourier_out = fourier_out.reshape(pair_count, 2, feat_width, 2, LAT)

    def forward_pair(bundle):
        pair_table, coeffs, side_rows = bundle
        both_sides = jnp.einsum('jl,skrl->sjkr', pair_table.astype(jnp.float32), coeffs.astype(jnp.float32))
        summed = lax.optimization_barrier(jnp.sum(jnp.where(side_rows[:, :, None, None], both_sides, 0.0), axis=0))
        return summed.reshape(degrees, channels).astype(jnp.bfloat16)
    return lax.map(forward_pair, (legendre, fourier_out, side_mask))
```

```python
import functools
import math

import jax
import jax.numpy as jnp
from jax import lax
from jax.experimental import pallas as pl
from jax.experimental.pallas import tpu as pltpu
from jax.sharding import PartitionSpec as P

NLON = 1280
FIELDS = 4
SPREAD = ((0.375, 0.625, 0.0), (0.125, 0.875, 0.0), (0.0, 0.875, 0.125), (0.0, 0.625, 0.375))
VMEM_BYTES = 56 * 1024 * 1024


def params():
    return pltpu.CompilerParams(vmem_limit_bytes=VMEM_BYTES)


def slot_waves(pair_low, wave_total):
    return jnp.stack([pair_low, wave_total - 1 - pair_low], axis=1).reshape(-1)


def slot_positions(regimes, experts_total):
    onehot = (regimes[:, None] == jnp.arange(experts_total, dtype=jnp.int32)).astype(jnp.int32)
    ranking = jnp.cumsum(onehot, axis=0) - 1
    return jnp.sum(ranking * onehot, axis=1)


def zonal_tables(pair_low, wave_total, devices):
    waves = slot_waves(pair_low, wave_total).reshape(devices, 1, -1)
    quarter = jnp.array([0, NLON // 4], jnp.int32).reshape(1, 2, 1)
    rows = (devices, 2, waves.shape[2])
    waves_k = jnp.broadcast_to(waves, rows).reshape(-1)
    turn_k = jnp.broadcast_to(quarter, rows).reshape(-1)
    order = jnp.arange(NLON, dtype=jnp.int32)
    longitude = 4 * (order % (NLON // 4)) + order // (NLON // 4)

    def cosines(wave, turn, lon):
        phases = (wave * lon + turn) % NLON
        return jnp.cos(phases.astype(jnp.float32) * jnp.float32(2.0 * math.pi / NLON))

    scale = jnp.where(waves_k == 0, jnp.float32(1.0), jnp.float32(2.0))
    inverse = cosines(waves_k[None, :], turn_k[None, :], longitude[:, None]) * scale[None, :]
    forward = cosines(waves_k[:, None], turn_k[:, None], longitude[None, :]) * jnp.float32(
        1.0 / math.sqrt(NLON)
    )
    return inverse.astype(jnp.bfloat16), forward.astype(jnp.bfloat16)


def split_matrix(width):
    channel = jnp.arange(width, dtype=jnp.int32)
    target = (channel % 2) * (width // 2) + channel // 2
    return (target[:, None] == channel[None, :]).astype(jnp.bfloat16)


def group_of(count):
    return max(size for size in range(1, 6) if count % size == 0)


def inverse_legendre_kernel(pairs, lats, low, spec, leg, split, out, held):
    step = pl.program_id(0)
    group, degrees, channels = spec.shape
    feat = channels // 2
    lat_total = leg.shape[1]
    middle = (degrees - 1) // 2
    skip = middle // 256 * 256
    pair_steps = pairs // group

    @pl.when(step < pair_steps)
    def _():
        for g in range(group):
            pair = step * group + g
            lower = degrees - 1 - low[pair]
            coeffs = jnp.dot(spec[g], split[...], preferred_element_type=jnp.float32)
            tail = coeffs[middle:]
            on_first = lax.broadcasted_iota(jnp.int32, tail.shape, 0) < lower - middle
            first = jnp.concatenate([coeffs[:middle], jnp.where(on_first, tail, 0.0)], axis=0)
            second = jnp.concatenate(
                [jnp.zeros((middle - skip, channels), jnp.float32), jnp.where(on_first, 0.0, tail)],
                axis=0,
            )
            sides = (
                jnp.dot(leg[g], first.astype(jnp.bfloat16), preferred_element_type=jnp.float32),
                jnp.dot(
                    leg[g, :, skip:],
                    second.astype(jnp.bfloat16),
                    preferred_element_type=jnp.float32,
                ),
            )
            for s in range(2):
                for r in range(2):
                    start = (r * 2 * pairs + 2 * pair + s) * lat_total
                    held[pl.ds(pl.multiple_of(start, 8), lat_total), :] = sides[s][
                        :, r * feat : (r + 1) * feat
                    ]

    @pl.when(step >= pair_steps)
    def _():
        for d in range(out.shape[0]):
            first_lat = ((step - pair_steps) * out.shape[0] + d) * lats
            for a in range(lats):
                rows = held[pl.ds(first_lat + a, 4 * pairs, stride=lat_total), :]
                out[d, :, a * feat : (a + 1) * feat] = rows.astype(jnp.bfloat16)


def inverse_legendre(spectral, legendre, local_low, devices):
    pairs, degrees, channels = spectral.shape
    lat_total = legendre.shape[1]
    lats = lat_total // devices
    feat = channels // 2
    group, batch = group_of(pairs), group_of(devices)
    pair_steps = pairs // group
    last = pair_steps - 1
    return pl.pallas_call(
        functools.partial(inverse_legendre_kernel, pairs, lats),
        grid=(pair_steps + devices // batch,),
        in_specs=[
            pl.BlockSpec(memory_space=pltpu.SMEM),
            pl.BlockSpec((group, degrees, channels), lambda i: (jnp.minimum(i, last), 0, 0)),
            pl.BlockSpec((group, lat_total, degrees), lambda i: (jnp.minimum(i, last), 0, 0)),
            pl.BlockSpec((channels, channels), lambda i: (0, 0)),
        ],
        out_specs=pl.BlockSpec(
            (batch, 4 * pairs, lats * feat), lambda i: (jnp.maximum(i - pair_steps, 0), 0, 0)
        ),
        out_shape=jax.ShapeDtypeStruct((devices, 4 * pairs, lats * feat), jnp.bfloat16),
        scratch_shapes=[pltpu.VMEM((4 * pairs * lat_total, feat), jnp.float32)],
        compiler_params=params(),
        name="inverse_legendre",
    )(local_low, spectral, legendre, split_matrix(channels))


def to_grid_kernel(slots, table, coeffs, forced, packed, cols, sent):
    step = pl.program_id(0)
    quarter, feat = cols.shape[1:]

    @pl.when(step == 0)
    def _():
        sent[...] = jnp.zeros_like(sent)

    grid = jnp.dot(table[...], coeffs[...], preferred_element_type=jnp.float32)
    total = jnp.zeros((quarter, feat), jnp.float32)
    for t in range(2):
        field = grid[:, t * feat : (t + 1) * feat]
        forced[:, t * feat : (t + 1) * feat] = field * pltpu.roll(
            field, feat - feat // FIELDS, axis=1
        )
        for u in range(4):
            total = total + field[u * quarter : (u + 1) * quarter]
    before = jnp.maximum(step - 1, 0) * quarter
    held = cols.at[(step + 1) % 2]
    for k in range(quarter):
        sent[pl.ds(slots[before + k], 1), :] = held[pl.ds(k, 1), :]
    cols[step % 2] = (total * 0.125).astype(jnp.bfloat16).astype(jnp.float32)

    @pl.when(step == pl.num_programs(0) - 1)
    def _():
        for k in range(quarter):
            sent[pl.ds(slots[step * quarter + k], 1), :] = cols[step % 2, pl.ds(k, 1), :]
        packed[...] = sent[...].astype(jnp.bfloat16)


def to_grid(slots, table, coeffs, slot_total, feat):
    depth, lanes = coeffs.shape
    rows = lanes // (2 * feat)
    return pl.pallas_call(
        to_grid_kernel,
        grid_spec=pltpu.PrefetchScalarGridSpec(
            num_scalar_prefetch=1,
            grid=(rows,),
            in_specs=[
                pl.BlockSpec((NLON, depth), lambda i, s: (0, 0)),
                pl.BlockSpec((depth, 2 * feat), lambda i, s: (0, i)),
            ],
            out_specs=[
                pl.BlockSpec((NLON, 2 * feat), lambda i, s: (0, i)),
                pl.BlockSpec((slot_total, feat), lambda i, s: (0, 0)),
            ],
            scratch_shapes=[
                pltpu.VMEM((2, NLON // 4, feat), jnp.float32),
                pltpu.VMEM((slot_total, feat), jnp.float32),
            ],
        ),
        out_shape=[
            jax.ShapeDtypeStruct((NLON, lanes), jnp.float32),
            jax.ShapeDtypeStruct((slot_total, feat), jnp.bfloat16),
        ],
        compiler_params=params(),
        name="to_grid",
    )(slots, table, coeffs)


def silu(v):
    return 0.5 * v * (1.0 + jnp.tanh(0.5 * v))


def network_kernel(cols, weight_in, weight_mid, weight_out, out):
    rows = out.shape[0] // 2
    for half in range(2):
        own = slice(half * rows, (half + 1) * rows)
        hidden = jnp.dot(cols[own], weight_in[...], preferred_element_type=jnp.float32)
        hidden = silu(hidden).astype(jnp.bfloat16)
        deeper = jnp.dot(hidden, weight_mid[...], preferred_element_type=jnp.float32)
        deeper = silu(deeper).astype(jnp.bfloat16)
        result = jnp.dot(deeper, weight_out[...], preferred_element_type=jnp.float32)
        out[own] = result.astype(jnp.bfloat16)


def network(columns, weight_in, weight_mid, weight_out):
    rows, feat = columns.shape
    hid = weight_in.shape[1]
    block = rows // 8
    return pl.pallas_call(
        network_kernel,
        grid=(rows // block,),
        in_specs=[
            pl.BlockSpec((block, feat), lambda i: (i, 0)),
            pl.BlockSpec((feat, hid), lambda i: (0, 0)),
            pl.BlockSpec((hid, hid), lambda i: (0, 0)),
            pl.BlockSpec((hid, feat), lambda i: (0, 0)),
        ],
        out_specs=pl.BlockSpec((block, feat), lambda i: (i, 0)),
        out_shape=jax.ShapeDtypeStruct((rows, feat), jnp.bfloat16),
        compiler_params=params(),
        name="network",
    )(columns, weight_in, weight_mid, weight_out)


def to_waves_kernel(slots, table, forced, answers, out, wide, cols, tend):
    step = pl.program_id(0)
    quarter, feat = cols.shape[1:]

    @pl.when(step == 0)
    def _():
        wide[...] = answers[...].astype(jnp.float32)
        for k in range(quarter):
            cols[0, pl.ds(k, 1), :] = wide[pl.ds(slots[k], 1), :]

    coarse = cols[step % 2]
    after = jnp.minimum(step + 1, pl.num_programs(0) - 1) * quarter
    held = cols.at[(step + 1) % 2]
    for k in range(quarter):
        held[pl.ds(k, 1), :] = wide[pl.ds(slots[after + k], 1), :]
    before = pltpu.roll(coarse, 1, axis=0)
    following = pltpu.roll(coarse, quarter - 1, axis=0)
    for u in range(4):
        w, v, x = SPREAD[u]
        fine = v * coarse + (w * before if w else x * following)
        rows = slice(u * quarter, (u + 1) * quarter)
        for t in range(2):
            lanes = slice(t * feat, (t + 1) * feat)
            tend[rows, lanes] = (forced[rows, lanes] + fine).astype(jnp.bfloat16)
    out[...] = jnp.dot(table[...], tend[...], preferred_element_type=jnp.float32).astype(
        jnp.bfloat16
    )


def to_waves(slots, table, forced, answers):
    lanes = forced.shape[1]
    slot_total, feat = answers.shape
    depth = table.shape[0]
    rows = lanes // (2 * feat)
    return pl.pallas_call(
        to_waves_kernel,
        grid_spec=pltpu.PrefetchScalarGridSpec(
            num_scalar_prefetch=1,
            grid=(rows,),
            in_specs=[
                pl.BlockSpec((depth, NLON), lambda i, s: (0, 0)),
                pl.BlockSpec((NLON, 2 * feat), lambda i, s: (0, i)),
                pl.BlockSpec((slot_total, feat), lambda i, s: (0, 0)),
            ],
            out_specs=pl.BlockSpec((depth, 2 * feat), lambda i, s: (0, i)),
            scratch_shapes=[
                pltpu.VMEM((slot_total, feat), jnp.float32),
                pltpu.VMEM((2, NLON // 4, feat), jnp.float32),
                pltpu.VMEM((NLON, 2 * feat), jnp.bfloat16),
            ],
        ),
        out_shape=jax.ShapeDtypeStruct((depth, lanes), jnp.bfloat16),
        compiler_params=params(),
        name="to_waves",
    )(slots, table, forced, answers)


def forward_legendre_kernel(lats, low, coeffs, leg, merge, out, held):
    step = pl.program_id(0)
    group, degrees, channels = out.shape
    feat = channels // 2
    lat_total = leg.shape[2]
    batch, rows = coeffs.shape[:2]
    lat_steps = lat_total // (batch * lats)
    middle = (degrees - 1) // 2

    @pl.when(step < lat_steps)
    def _():
        for d in range(batch):
            first_lat = (step * batch + d) * lats
            for a in range(lats):
                held[pl.ds(first_lat + a, rows, stride=lat_total), :] = coeffs[
                    d, :, a * feat : (a + 1) * feat
                ].astype(jnp.float32)

    @pl.when(step >= lat_steps)
    def _():
        for g in range(group):
            pair = (step - lat_steps) * group + g
            lower = degrees - 1 - low[pair]
            sides = []
            for s in range(2):
                parts = []
                for r in range(2):
                    start = (r * (rows // 2) + 2 * pair + s) * lat_total
                    parts.append(held[pl.ds(pl.multiple_of(start, 8), lat_total), :])
                sides.append(jnp.concatenate(parts, axis=1).astype(jnp.bfloat16))
            first = jnp.dot(leg[g], sides[0], preferred_element_type=jnp.float32)
            second = jnp.dot(leg[g, middle:], sides[1], preferred_element_type=jnp.float32)
            on_first = lax.broadcasted_iota(jnp.int32, second.shape, 0) < lower - middle
            chosen = jnp.concatenate(
                [first[:middle], jnp.where(on_first, first[middle:], second)], axis=0
            )
            out[g] = jnp.dot(
                chosen.astype(jnp.bfloat16), merge[...], preferred_element_type=jnp.float32
            ).astype(jnp.bfloat16)


def forward_legendre(coeffs, legendre, local_low, channels):
    devices, rows, lanes = coeffs.shape
    pairs, degrees, lat_total = legendre.shape
    feat = channels // 2
    lats = lat_total // devices
    group, batch = group_of(pairs), group_of(devices)
    lat_steps = devices // batch
    return pl.pallas_call(
        functools.partial(forward_legendre_kernel, lats),
        grid=(lat_steps + pairs // group,),
        in_specs=[
            pl.BlockSpec(memory_space=pltpu.SMEM),
            pl.BlockSpec((batch, rows, lanes), lambda i: (jnp.minimum(i, lat_steps - 1), 0, 0)),
            pl.BlockSpec(
                (group, degrees, lat_total), lambda i: (jnp.maximum(i - lat_steps, 0), 0, 0)
            ),
            pl.BlockSpec((channels, channels), lambda i: (0, 0)),
        ],
        out_specs=pl.BlockSpec(
            (group, degrees, channels), lambda i: (jnp.maximum(i - lat_steps, 0), 0, 0)
        ),
        out_shape=jax.ShapeDtypeStruct((pairs, degrees, channels), jnp.bfloat16),
        scratch_shapes=[pltpu.VMEM((rows * lat_total, feat), jnp.float32)],
        compiler_params=params(),
        name="forward_legendre",
    )(local_low, coeffs, legendre, split_matrix(channels).T)


def exchange(blocks):
    return lax.all_to_all(blocks, "wave", split_axis=0, concat_axis=0, tiled=True)


def on_device(spectral, legendre, pair_low, routes, w_in, w_mid, w_out):
    pairs, degrees, channels = spectral.shape
    feat = channels // 2
    devices = lax.axis_size("wave")
    local_low = lax.dynamic_slice_in_dim(pair_low, lax.axis_index("wave") * pairs, pairs)

    sent = inverse_legendre(spectral, jnp.swapaxes(legendre, 1, 2), local_low, devices)
    arrived = exchange(sent)
    inverse_table, forward_table = zonal_tables(pair_low, degrees - 1, devices)
    regimes = routes[:, 0]
    capacity = 2 * regimes.shape[0] // devices
    slots = regimes * capacity + slot_positions(regimes, devices)

    forced, outgoing = to_grid(
        slots, inverse_table, arrived.reshape(-1, arrived.shape[2]), devices * capacity, feat
    )
    columns = exchange(outgoing.reshape(devices, capacity, feat))
    answers = network(columns.reshape(-1, feat), w_in[0], w_mid[0], w_out[0])
    incoming = exchange(answers.reshape(devices, capacity, feat)).reshape(-1, feat)
    waves = to_waves(slots, forward_table, forced, incoming)
    received = exchange(waves.reshape(arrived.shape))
    return forward_legendre(received, legendre, local_low, channels)


def solution(mesh):
    placed = (
        P(("grp", "wave"), None, None),
        P("wave", None, None),
        P(),
        P(("grp", "wave"), None),
        P("wave", None, None),
        P("wave", None, None),
        P("wave", None, None),
    )
    return jax.shard_map(
        on_device,
        mesh=mesh,
        in_specs=placed,
        out_specs=P(("grp", "wave"), None, None),
        check_vma=False,
    )
```

```python
import functools
import math

import jax
import jax.numpy as jnp
from jax import lax
from jax.experimental import pallas as pl
from jax.experimental.pallas import tpu as pltpu
from jax.sharding import PartitionSpec as P

NLON = 1280
FIELDS = 4
SPREAD = ((0.375, 0.625, 0.0), (0.125, 0.875, 0.0), (0.0, 0.875, 0.125), (0.0, 0.625, 0.375))
PITCH_EXTRA = 8


def params(mebibytes):
    return pltpu.CompilerParams(vmem_limit_bytes=mebibytes * 1024 * 1024)


def slot_positions(regimes, experts_total):
    onehot = (regimes[:, None] == jnp.arange(experts_total, dtype=jnp.int32)).astype(jnp.int32)
    ranking = jnp.cumsum(onehot, axis=0) - 1
    return jnp.sum(ranking * onehot, axis=1)


def zonal_tables(pair_low, wave_total):
    other = wave_total - 1 - pair_low
    even = jnp.where(pair_low % 2 == 0, pair_low, other)
    waves = jnp.stack([even, wave_total - 1 - even]).reshape(2, -1, 1)
    quarter = jnp.array([0, NLON // 4], jnp.int32).reshape(1, 1, 2)
    rows = (2, waves.shape[1], 2)
    waves_k = jnp.broadcast_to(waves, rows).reshape(2, -1)
    turn_k = jnp.broadcast_to(quarter, rows).reshape(2, -1)
    order = jnp.arange(NLON // 2, dtype=jnp.int32)
    longitude = 4 * (order % (NLON // 8)) + order // (NLON // 8)

    def cosines(wave, turn, lon):
        phases = (wave * lon + turn) % NLON
        return jnp.cos(phases.astype(jnp.float32) * jnp.float32(2.0 * math.pi / NLON))

    scale = jnp.where(waves_k == 0, jnp.float32(1.0), jnp.float32(2.0))
    inverse = scale[:, None, :] * cosines(
        waves_k[:, None, :], turn_k[:, None, :], longitude[None, :, None]
    )
    forward = jnp.float32(1.0 / math.sqrt(NLON)) * cosines(
        waves_k[:, :, None], turn_k[:, :, None], longitude[None, None, :]
    )
    return inverse.astype(jnp.bfloat16), forward.astype(jnp.bfloat16)


def lats_together(lats):
    return 4 if lats % 4 == 0 else 2


def lane_start(lat, parity, lats, feat):
    together = lats_together(lats)
    return ((lat // together * 2 + parity) * together + lat % together) * feat


def in_vmem(array):
    return pltpu.with_memory_space_constraint(array, pltpu.VMEM)


WHOLE = pl.BlockSpec(memory_space=pltpu.VMEM)


def split_matrix(width):
    channel = jnp.arange(width, dtype=jnp.int32)
    target = (channel % 2) * (width // 2) + channel // 2
    return (target[:, None] == channel[None, :]).astype(jnp.bfloat16)


def group_of(pairs):
    return 4 if pairs % 4 == 0 else pairs


def staggered(step, steps, first, second, slots):
    @pl.when(step == 0)
    def _():
        first(0, slots[0])

    for odd in range(2):

        @pl.when((step > 0) & (step < steps) & (step % 2 == odd))
        def _(odd=odd):
            second(step - 1, slots[1 - odd])
            first(step, slots[odd])

    @pl.when(step == steps)
    def _():
        second(steps - 1, slots[(steps - 1) % 2])


def inverse_legendre_kernel(steps, low, spec, leg, split, out, *slots):
    step = pl.program_id(0)
    group, degrees, channels = spec.shape
    feat = channels // 2
    lat_total = leg.shape[1]
    devices, rows = out.shape[:2]
    lats = lat_total // devices
    pitch = lat_total + PITCH_EXTRA
    middle = (degrees - 1) // 2
    skip = middle // 256 * 256

    def transform(number, held):
        for g in range(group):
            own_low = low[number * group + g]
            lower = degrees - 1 - own_low
            coeffs = jnp.dot(spec[g], split[...], preferred_element_type=jnp.float32)
            tail = coeffs[middle:]
            on_first = lax.broadcasted_iota(jnp.int32, tail.shape, 0) < lower - middle
            first = jnp.concatenate([coeffs[:middle], jnp.where(on_first, tail, 0.0)], axis=0)
            second = jnp.concatenate(
                [jnp.zeros((middle - skip, channels), jnp.float32), jnp.where(on_first, 0.0, tail)],
                axis=0,
            )
            sides = (
                jnp.dot(leg[g], first.astype(jnp.bfloat16), preferred_element_type=jnp.float32),
                jnp.dot(
                    leg[g, :, skip:],
                    second.astype(jnp.bfloat16),
                    preferred_element_type=jnp.float32,
                ),
            )
            for s in range(2):
                parity = (own_low + s) % 2
                for r in range(2):
                    start = (parity * rows + 2 * g + r) * pitch
                    held[pl.ds(pl.multiple_of(start, 8), lat_total), :] = sides[s][
                        :, r * feat : (r + 1) * feat
                    ]

    def turn(_, held):
        for d in range(devices):
            for a in range(lats):
                for parity in range(2):
                    start = parity * rows * pitch + d * lats + a
                    own = held[pl.ds(start, rows, stride=pitch), :]
                    lane = lane_start(a, parity, lats, feat)
                    out[d, :, lane : lane + feat] = own.astype(jnp.bfloat16)

    staggered(step, steps, transform, turn, slots)


def inverse_legendre(spectral, legendre, local_low, devices):
    pairs, degrees, channels = spectral.shape
    lat_total = legendre.shape[1]
    lanes = lat_total // devices * channels
    group = group_of(pairs)
    steps = pairs // group
    slot = pltpu.VMEM((4 * group * (lat_total + PITCH_EXTRA), channels // 2), jnp.float32)
    return pl.pallas_call(
        functools.partial(inverse_legendre_kernel, steps),
        grid=(steps + 1,),
        in_specs=[
            pl.BlockSpec(memory_space=pltpu.SMEM),
            pl.BlockSpec((group, degrees, channels), lambda i: (jnp.minimum(i, steps - 1), 0, 0)),
            pl.BlockSpec((group, lat_total, degrees), lambda i: (jnp.minimum(i, steps - 1), 0, 0)),
            pl.BlockSpec((channels, channels), lambda i: (0, 0)),
        ],
        out_specs=pl.BlockSpec(
            (devices, 2 * group, lanes), lambda i: (0, jnp.maximum(i - 1, 0), 0)
        ),
        out_shape=jax.ShapeDtypeStruct((devices, 2 * pairs, lanes), jnp.bfloat16),
        scratch_shapes=[slot, slot],
        compiler_params=params(40),
        name="inverse_legendre",
    )(local_low, spectral, legendre, split_matrix(channels))


def to_grid_kernel(steps, slots, table, coeffs, forced, packed, cols, sent, *held):
    step = pl.program_id(0)
    count, feat = cols.shape
    lanes = forced.shape[2]
    half = table.shape[1]
    eighth = half // 4
    lat_rows = lanes // (2 * feat)

    def transform(number, parts):
        for parity in range(2):
            start = pl.multiple_of((2 * number + parity) * lanes, lanes)
            parts[parity] = jnp.dot(
                table[parity],
                coeffs[:, pl.ds(start, lanes)],
                preferred_element_type=jnp.float32,
            )

    def finish(number, parts):
        for i in range(lat_rows):
            totals = [jnp.zeros((eighth, feat), jnp.float32) for _ in range(2)]
            for t in (2 * i, 2 * i + 1):
                own = slice(t * feat, (t + 1) * feat)
                for u in range(4):
                    rows = slice(u * eighth, (u + 1) * eighth)
                    even, odd = parts[0, rows, own], parts[1, rows, own]
                    for h, field in enumerate((even + odd, even - odd)):
                        totals[h] = totals[h] + field
                        start = h * half + u * eighth
                        forced[number, start : start + eighth, own] = field * pltpu.roll(
                            field, feat - feat // FIELDS, axis=1
                        )
            for h in range(2):
                start = (2 * i + h) * eighth
                cols[start : start + eighth, :] = (
                    (totals[h] * 0.125).astype(jnp.bfloat16).astype(jnp.float32)
                )
        for k in range(count):
            sent[pl.ds(slots[number * count + k], 1), :] = cols[pl.ds(k, 1), :]

    @pl.when(step == 0)
    def _():
        sent[...] = jnp.zeros_like(sent)

    staggered(step, steps, transform, finish, held)

    @pl.when(step == steps)
    def _():
        packed[...] = sent[...].astype(jnp.bfloat16)


def to_grid(slots, table, coeffs, slot_total, feat):
    depth, lanes = coeffs.shape
    lats = lanes // (2 * feat)
    together = lats_together(lats)
    own = together * feat
    count = together // 2 * (NLON // 4)
    steps = lats // together
    part = pltpu.VMEM((2, NLON // 2, own), jnp.float32)
    return pl.pallas_call(
        functools.partial(to_grid_kernel, steps),
        grid_spec=pltpu.PrefetchScalarGridSpec(
            num_scalar_prefetch=1,
            grid=(steps + 1,),
            in_specs=[
                pl.BlockSpec((2, NLON // 2, depth), lambda i, s: (0, 0, 0)),
                WHOLE,
            ],
            out_specs=[WHOLE, pl.BlockSpec((slot_total, feat), lambda i, s: (0, 0))],
            scratch_shapes=[
                pltpu.VMEM((count, feat), jnp.float32),
                pltpu.VMEM((slot_total, feat), jnp.float32),
                part,
                part,
            ],
        ),
        out_shape=[
            pltpu.VMEM((steps, NLON, own), jnp.float32),
            jax.ShapeDtypeStruct((slot_total, feat), jnp.bfloat16),
        ],
        compiler_params=params(30),
        name="to_grid",
    )(slots, table, in_vmem(coeffs))


def silu(v):
    return 0.5 * v * (1.0 + jnp.tanh(0.5 * v))


def network_kernel(cols, weight_in, weight_mid, weight_out, out):
    rows = out.shape[0] // 2
    for half in range(2):
        own = slice(half * rows, (half + 1) * rows)
        hidden = jnp.dot(cols[own], weight_in[...], preferred_element_type=jnp.float32)
        hidden = silu(hidden).astype(jnp.bfloat16)
        deeper = jnp.dot(hidden, weight_mid[...], preferred_element_type=jnp.float32)
        deeper = silu(deeper).astype(jnp.bfloat16)
        result = jnp.dot(deeper, weight_out[...], preferred_element_type=jnp.float32)
        out[own] = result.astype(jnp.bfloat16)


def network(columns, weight_in, weight_mid, weight_out):
    rows, feat = columns.shape
    hid = weight_in.shape[1]
    block = rows // 8
    return pl.pallas_call(
        network_kernel,
        grid=(rows // block,),
        in_specs=[
            pl.BlockSpec((block, feat), lambda i: (i, 0)),
            pl.BlockSpec((feat, hid), lambda i: (0, 0)),
            pl.BlockSpec((hid, hid), lambda i: (0, 0)),
            pl.BlockSpec((hid, feat), lambda i: (0, 0)),
        ],
        out_specs=pl.BlockSpec((block, feat), lambda i: (i, 0)),
        out_shape=jax.ShapeDtypeStruct((rows, feat), jnp.bfloat16),
        compiler_params=params(30),
        name="network",
    )(columns, weight_in, weight_mid, weight_out)


def to_waves_kernel(steps, slots, table, forced, answers, out, wide, *held):
    step = pl.program_id(0)
    count, feat = held[1].shape
    lanes = forced.shape[2]
    half = table.shape[2]
    eighth = half // 4
    quarter = 2 * eighth

    def collect(number, cols):
        for k in range(count):
            cols[pl.ds(k, 1), :] = wide[pl.ds(slots[number * count + k], 1), :]

    def fold(number, slot):
        folded, cols, next_cols = slot
        for i in range(count // quarter):
            coarse = cols[i * quarter : (i + 1) * quarter, :]
            before = pltpu.roll(coarse, 1, axis=0)
            following = pltpu.roll(coarse, quarter - 1, axis=0)
            for u in range(4):
                w, v, x = SPREAD[u]
                fine = v * coarse + (w * before if w else x * following)
                rows = slice(u * eighth, (u + 1) * eighth)
                far_rows = slice(half + u * eighth, half + (u + 1) * eighth)
                for t in (2 * i, 2 * i + 1):
                    own = slice(t * feat, (t + 1) * feat)
                    near = forced[number, rows, own] + fine[:eighth]
                    far = forced[number, far_rows, own] + fine[eighth:]
                    folded[0, rows, own] = (near + far).astype(jnp.bfloat16)
                    folded[1, rows, own] = (near - far).astype(jnp.bfloat16)
        collect(jnp.minimum(number + 1, steps - 1), next_cols)

    def transform(_, slot):
        folded = slot[0]
        for parity in range(2):
            out[:, parity * lanes : (parity + 1) * lanes] = jnp.dot(
                table[parity], folded[parity], preferred_element_type=jnp.float32
            ).astype(jnp.bfloat16)

    @pl.when(step == 0)
    def _():
        wide[...] = answers[...].astype(jnp.float32)
        collect(0, held[1])

    staggered(
        step,
        steps,
        fold,
        transform,
        ((held[0], held[1], held[3]), (held[2], held[3], held[1])),
    )


def to_waves(slots, table, forced, answers):
    steps, _, own = forced.shape
    slot_total, feat = answers.shape
    depth = table.shape[1]
    count = own // feat // 2 * (NLON // 4)
    slot = [
        pltpu.VMEM((2, NLON // 2, own), jnp.bfloat16),
        pltpu.VMEM((count, feat), jnp.float32),
    ]
    return pl.pallas_call(
        functools.partial(to_waves_kernel, steps),
        grid_spec=pltpu.PrefetchScalarGridSpec(
            num_scalar_prefetch=1,
            grid=(steps + 1,),
            in_specs=[
                pl.BlockSpec((2, depth, NLON // 2), lambda i, s: (0, 0, 0)),
                WHOLE,
                pl.BlockSpec((slot_total, feat), lambda i, s: (0, 0)),
            ],
            out_specs=pl.BlockSpec((depth, 2 * own), lambda i, s: (0, jnp.maximum(i - 1, 0))),
            scratch_shapes=[
                pltpu.VMEM((slot_total, feat), jnp.float32),
                *slot,
                *slot,
            ],
        ),
        out_shape=jax.ShapeDtypeStruct((depth, 2 * steps * own), jnp.bfloat16),
        compiler_params=params(30),
        name="to_waves",
    )(slots, table, in_vmem(forced), answers)


def forward_legendre_kernel(steps, low, coeffs, leg, merge, out, *slots):
    step = pl.program_id(0)
    group, degrees, channels = out.shape
    feat = channels // 2
    lat_total = leg.shape[2]
    devices, rows = coeffs.shape[0], 2 * group
    lats = lat_total // devices
    pitch = lat_total + PITCH_EXTRA
    middle = (degrees - 1) // 2

    def turn(number, held):
        own_rows = slice(None)
        if coeffs.shape[1] > rows:
            own_rows = pl.ds(pl.multiple_of(number * rows, rows), rows)
        for d in range(devices):
            for a in range(lats):
                for parity in range(2):
                    start = parity * rows * pitch + d * lats + a
                    lane = lane_start(a, parity, lats, feat)
                    held[pl.ds(start, rows, stride=pitch), :] = coeffs[
                        d, own_rows, lane : lane + feat
                    ].astype(jnp.float32)

    def transform(number, held):
        for g in range(group):
            own_low = low[number * group + g]
            lower = degrees - 1 - own_low
            sides = []
            for s in range(2):
                parity = (own_low + s) % 2
                parts = []
                for r in range(2):
                    start = (parity * rows + 2 * g + r) * pitch
                    parts.append(held[pl.ds(pl.multiple_of(start, 8), lat_total), :])
                sides.append(jnp.concatenate(parts, axis=1).astype(jnp.bfloat16))
            first = jnp.dot(leg[number * group + g], sides[0], preferred_element_type=jnp.float32)
            second = jnp.dot(leg[number * group + g, middle:], sides[1], preferred_element_type=jnp.float32)
            on_first = lax.broadcasted_iota(jnp.int32, second.shape, 0) < lower - middle
            chosen = jnp.concatenate(
                [first[:middle], jnp.where(on_first, first[middle:], second)], axis=0
            )
            out[g] = jnp.dot(
                chosen.astype(jnp.bfloat16), merge[...], preferred_element_type=jnp.float32
            ).astype(jnp.bfloat16)

    staggered(step, steps, turn, transform, slots)


def forward_legendre(coeffs, legendre, local_low, channels):
    devices, rows, lanes = coeffs.shape
    pairs, degrees, lat_total = legendre.shape
    group = group_of(pairs)
    steps = pairs // group
    slot = pltpu.VMEM((4 * group * (lat_total + PITCH_EXTRA), channels // 2), jnp.float32)
    return pl.pallas_call(
        functools.partial(forward_legendre_kernel, steps),
        grid=(steps + 1,),
        in_specs=[
            pl.BlockSpec(memory_space=pltpu.SMEM),
            WHOLE,
            WHOLE,
            pl.BlockSpec((channels, channels), lambda i: (0, 0)),
        ],
        out_specs=pl.BlockSpec((group, degrees, channels), lambda i: (jnp.maximum(i - 1, 0), 0, 0)),
        out_shape=jax.ShapeDtypeStruct((pairs, degrees, channels), jnp.bfloat16),
        scratch_shapes=[slot, slot],
        compiler_params=params(30),
        name="forward_legendre",
    )(local_low, in_vmem(coeffs), in_vmem(legendre), split_matrix(channels).T)


def exchange(blocks):
    return lax.all_to_all(blocks, "wave", split_axis=0, concat_axis=0, tiled=True)


def on_device(spectral, legendre, pair_low, routes, w_in, w_mid, w_out):
    pairs, degrees, channels = spectral.shape
    feat = channels // 2
    devices = lax.axis_size("wave")
    local_low = lax.dynamic_slice_in_dim(pair_low, lax.axis_index("wave") * pairs, pairs)

    sent = inverse_legendre(spectral, jnp.swapaxes(legendre, 1, 2), local_low, devices)
    arrived = exchange(sent)
    inverse_table, forward_table = zonal_tables(pair_low, degrees - 1)
    regimes = routes[:, 0]
    capacity = 2 * regimes.shape[0] // devices
    slots = regimes * capacity + slot_positions(regimes, devices)

    forced, outgoing = to_grid(
        slots, inverse_table, arrived.reshape(-1, arrived.shape[2]), devices * capacity, feat
    )
    columns = exchange(outgoing.reshape(devices, capacity, feat))
    answers = network(columns.reshape(-1, feat), w_in[0], w_mid[0], w_out[0])
    incoming = exchange(answers.reshape(devices, capacity, feat)).reshape(-1, feat)
    waves = to_waves(slots, forward_table, forced, incoming)
    received = exchange(waves.reshape(arrived.shape))
    return forward_legendre(received, legendre, local_low, channels)


def solution(mesh):
    placed = (
        P(("grp", "wave"), None, None),
        P("wave", None, None),
        P(),
        P(("grp", "wave"), None),
        P("wave", None, None),
        P("wave", None, None),
        P("wave", None, None),
    )
    return jax.shard_map(
        on_device,
        mesh=mesh,
        in_specs=placed,
        out_specs=P(("grp", "wave"), None, None),
        check_vma=False,
    )
```

```python
import functools
import itertools
import math

import jax
import jax.numpy as jnp
from jax import lax
from jax.experimental import pallas as pl
from jax.experimental.pallas import tpu as pltpu
from jax.sharding import PartitionSpec as P

NLON = 1280
FIELDS = 4
SPREAD = ((0.375, 0.625, 0.0), (0.125, 0.875, 0.0), (0.0, 0.875, 0.125), (0.0, 0.625, 0.375))
PITCH_EXTRA = 8
VMEM_BYTES = 56 * 1024 * 1024


def params():
    return pltpu.CompilerParams(vmem_limit_bytes=VMEM_BYTES)


def slot_positions(regimes, experts_total):
    onehot = (regimes[:, None] == jnp.arange(experts_total, dtype=jnp.int32)).astype(jnp.int32)
    ranking = jnp.cumsum(onehot, axis=0) - 1
    return jnp.sum(ranking * onehot, axis=1)


def zonal_tables(pair_low, wave_total):
    other = wave_total - 1 - pair_low
    even = jnp.where(pair_low % 2 == 0, pair_low, other)
    waves = jnp.stack([even, wave_total - 1 - even]).reshape(2, -1, 1)
    quarter = jnp.array([0, NLON // 4], jnp.int32).reshape(1, 1, 2)
    rows = (2, waves.shape[1], 2)
    waves_k = jnp.broadcast_to(waves, rows).reshape(2, -1)
    turn_k = jnp.broadcast_to(quarter, rows).reshape(2, -1)
    order = jnp.arange(NLON // 2, dtype=jnp.int32)
    longitude = 4 * (order % (NLON // 8)) + order // (NLON // 8)

    def cosines(wave, turn, lon):
        phases = (wave * lon + turn) % NLON
        return jnp.cos(phases.astype(jnp.float32) * jnp.float32(2.0 * math.pi / NLON))

    scale = jnp.where(waves_k == 0, jnp.float32(1.0), jnp.float32(2.0))
    inverse = scale[:, None, :] * cosines(
        waves_k[:, None, :], turn_k[:, None, :], longitude[None, :, None]
    )
    forward = jnp.float32(1.0 / math.sqrt(NLON)) * cosines(
        waves_k[:, :, None], turn_k[:, :, None], longitude[None, None, :]
    )
    return inverse.astype(jnp.bfloat16), forward.astype(jnp.bfloat16)


def lats_together(lats):
    return 4 if lats % 4 == 0 else 2


def lane_start(lat, parity, lats, feat):
    together = lats_together(lats)
    return ((lat // together * 2 + parity) * together + lat % together) * feat


def split_matrix(width):
    channel = jnp.arange(width, dtype=jnp.int32)
    target = (channel % 2) * (width // 2) + channel // 2
    return (target[:, None] == channel[None, :]).astype(jnp.bfloat16)


def group_of(pairs):
    return 4 if pairs % 4 == 0 else pairs


def staggered(step, steps, first, second, slots):
    def run(*parts):
        for _ in itertools.zip_longest(*parts):
            pass

    @pl.when(step == 0)
    def _():
        run(first(0, slots[0]))

    for odd in range(2):

        @pl.when((step > 0) & (step < steps) & (step % 2 == odd))
        def _(odd=odd):
            run(second(step - 1, slots[1 - odd]), first(step, slots[odd]))

    @pl.when(step == steps)
    def _():
        run(second(steps - 1, slots[(steps - 1) % 2]))


def inverse_legendre_kernel(steps, low, spec, leg, split, out, *slots):
    step = pl.program_id(0)
    group, degrees, channels = spec.shape
    feat = channels // 2
    lat_total = leg.shape[1]
    devices, rows = out.shape[:2]
    lats = lat_total // devices
    pitch = lat_total + PITCH_EXTRA
    middle = (degrees - 1) // 2
    skip = middle // 256 * 256

    def transform(number, held):
        for g in range(group):
            own_low = low[number * group + g]
            lower = degrees - 1 - own_low
            coeffs = jnp.dot(spec[g], split[...], preferred_element_type=jnp.float32)
            tail = coeffs[middle:]
            on_first = lax.broadcasted_iota(jnp.int32, tail.shape, 0) < lower - middle
            first = jnp.concatenate([coeffs[:middle], jnp.where(on_first, tail, 0.0)], axis=0)
            second = jnp.concatenate(
                [jnp.zeros((middle - skip, channels), jnp.float32), jnp.where(on_first, 0.0, tail)],
                axis=0,
            )
            sides = (
                jnp.dot(leg[g], first.astype(jnp.bfloat16), preferred_element_type=jnp.float32),
                jnp.dot(
                    leg[g, :, skip:],
                    second.astype(jnp.bfloat16),
                    preferred_element_type=jnp.float32,
                ),
            )
            for s in range(2):
                parity = (own_low + s) % 2
                for r in range(2):
                    start = (parity * rows + 2 * g + r) * pitch
                    held[pl.ds(pl.multiple_of(start, 8), lat_total), :] = sides[s][
                        :, r * feat : (r + 1) * feat
                    ]
            yield

    def turn(_, held):
        for d in range(devices):
            for a in range(lats):
                for parity in range(2):
                    start = parity * rows * pitch + d * lats + a
                    own = held[pl.ds(start, rows, stride=pitch), :]
                    lane = lane_start(a, parity, lats, feat)
                    out[d, :, lane : lane + feat] = own.astype(jnp.bfloat16)
            if (d + 1) % (devices // 4) == 0:
                yield

    staggered(step, steps, transform, turn, slots)


def inverse_legendre(spectral, legendre, local_low, devices):
    pairs, degrees, channels = spectral.shape
    lat_total = legendre.shape[1]
    lanes = lat_total // devices * channels
    group = group_of(pairs)
    steps = pairs // group
    slot = pltpu.VMEM((4 * group * (lat_total + PITCH_EXTRA), channels // 2), jnp.float32)
    return pl.pallas_call(
        functools.partial(inverse_legendre_kernel, steps),
        grid=(steps + 1,),
        in_specs=[
            pl.BlockSpec(memory_space=pltpu.SMEM),
            pl.BlockSpec((group, degrees, channels), lambda i: (jnp.minimum(i, steps - 1), 0, 0)),
            pl.BlockSpec((group, lat_total, degrees), lambda i: (jnp.minimum(i, steps - 1), 0, 0)),
            pl.BlockSpec((channels, channels), lambda i: (0, 0)),
        ],
        out_specs=pl.BlockSpec(
            (devices, 2 * group, lanes), lambda i: (0, jnp.maximum(i - 1, 0), 0)
        ),
        out_shape=jax.ShapeDtypeStruct((devices, 2 * pairs, lanes), jnp.bfloat16),
        scratch_shapes=[slot, slot],
        compiler_params=params(),
        name="inverse_legendre",
    )(local_low, spectral, legendre, split_matrix(channels))


def to_grid_kernel(steps, slots, table, coeffs, forced, packed, cols, sent, *held):
    step = pl.program_id(0)
    count, feat = cols.shape
    lanes = forced.shape[1]
    half = table.shape[1]
    eighth = half // 4
    lat_rows = lanes // (2 * feat)

    def transform(_, parts):
        for parity in range(2):
            for at in range(0, lanes, 2 * feat):
                start = parity * lanes + at
                parts[parity, :, at : at + 2 * feat] = jnp.dot(
                    table[parity],
                    coeffs[:, start : start + 2 * feat],
                    preferred_element_type=jnp.float32,
                )
                yield

    def finish(number, parts):
        for i in range(lat_rows):
            totals = [jnp.zeros((eighth, feat), jnp.float32) for _ in range(2)]
            for t in (2 * i, 2 * i + 1):
                own = slice(t * feat, (t + 1) * feat)
                for u in range(4):
                    rows = slice(u * eighth, (u + 1) * eighth)
                    even, odd = parts[0, rows, own], parts[1, rows, own]
                    for h, field in enumerate((even + odd, even - odd)):
                        totals[h] = totals[h] + field
                        start = h * half + u * eighth
                        product = field * pltpu.roll(field, feat - feat // FIELDS, axis=1)
                        forced[start : start + eighth, own] = product.astype(jnp.bfloat16)
                if t == 2 * i:
                    yield
            for h in range(2):
                start = (2 * i + h) * eighth
                cols[start : start + eighth, :] = (
                    (totals[h] * 0.125).astype(jnp.bfloat16).astype(jnp.float32)
                )
            for k in range(2 * i * eighth, 2 * (i + 1) * eighth):
                sent[pl.ds(slots[number * count + k], 1), :] = cols[pl.ds(k, 1), :]
            yield

    @pl.when(step == 0)
    def _():
        sent[...] = jnp.zeros_like(sent)

    staggered(step, steps, transform, finish, held)

    @pl.when(step == steps)
    def _():
        packed[...] = sent[...].astype(jnp.bfloat16)


def to_grid(slots, table, coeffs, slot_total, feat):
    depth, lanes = coeffs.shape
    lats = lanes // (2 * feat)
    together = lats_together(lats)
    own = together * feat
    count = together // 2 * (NLON // 4)
    steps = lats // together
    part = pltpu.VMEM((2, NLON // 2, own), jnp.float32)
    return pl.pallas_call(
        functools.partial(to_grid_kernel, steps),
        grid_spec=pltpu.PrefetchScalarGridSpec(
            num_scalar_prefetch=1,
            grid=(steps + 1,),
            in_specs=[
                pl.BlockSpec((2, NLON // 2, depth), lambda i, s: (0, 0, 0)),
                pl.BlockSpec((depth, 2 * own), lambda i, s: (0, jnp.minimum(i, steps - 1))),
            ],
            out_specs=[
                pl.BlockSpec((NLON, own), lambda i, s: (0, jnp.maximum(i - 1, 0))),
                pl.BlockSpec((slot_total, feat), lambda i, s: (0, 0)),
            ],
            scratch_shapes=[
                pltpu.VMEM((count, feat), jnp.float32),
                pltpu.VMEM((slot_total, feat), jnp.float32),
                part,
                part,
            ],
        ),
        out_shape=[
            jax.ShapeDtypeStruct((NLON, lats * feat), jnp.bfloat16),
            jax.ShapeDtypeStruct((slot_total, feat), jnp.bfloat16),
        ],
        compiler_params=params(),
        name="to_grid",
    )(slots, table, coeffs)


def silu(v):
    return 0.5 * v * (1.0 + jnp.tanh(0.5 * v))


def network_kernel(cols, weight_in, weight_mid, weight_out, out):
    rows = out.shape[0] // 2
    for half in range(2):
        own = slice(half * rows, (half + 1) * rows)
        hidden = jnp.dot(cols[own], weight_in[...], preferred_element_type=jnp.float32)
        hidden = silu(hidden).astype(jnp.bfloat16)
        deeper = jnp.dot(hidden, weight_mid[...], preferred_element_type=jnp.float32)
        deeper = silu(deeper).astype(jnp.bfloat16)
        result = jnp.dot(deeper, weight_out[...], preferred_element_type=jnp.float32)
        out[own] = result.astype(jnp.bfloat16)


def network(columns, weight_in, weight_mid, weight_out):
    rows, feat = columns.shape
    hid = weight_in.shape[1]
    block = rows // 8
    return pl.pallas_call(
        network_kernel,
        grid=(rows // block,),
        in_specs=[
            pl.BlockSpec((block, feat), lambda i: (i, 0)),
            pl.BlockSpec((feat, hid), lambda i: (0, 0)),
            pl.BlockSpec((hid, hid), lambda i: (0, 0)),
            pl.BlockSpec((hid, feat), lambda i: (0, 0)),
        ],
        out_specs=pl.BlockSpec((block, feat), lambda i: (i, 0)),
        out_shape=jax.ShapeDtypeStruct((rows, feat), jnp.bfloat16),
        compiler_params=params(),
        name="network",
    )(columns, weight_in, weight_mid, weight_out)


def to_waves_kernel(steps, slots, table, forced, answers, out, wide, *held):
    step = pl.program_id(0)
    count, feat = held[1].shape
    lanes = forced.shape[1]
    half = table.shape[2]
    eighth = half // 4
    quarter = 2 * eighth

    def collect(number, cols, start, size):
        for k in range(start, start + size):
            cols[pl.ds(k, 1), :] = wide[pl.ds(slots[number * count + k], 1), :]

    def fold(number, slot):
        folded, cols, next_cols = slot
        after = jnp.minimum(number + 1, steps - 1)
        for i in range(count // quarter):
            coarse = cols[i * quarter : (i + 1) * quarter, :]
            before = pltpu.roll(coarse, 1, axis=0)
            following = pltpu.roll(coarse, quarter - 1, axis=0)
            for u in range(4):
                w, v, x = SPREAD[u]
                fine = v * coarse + (w * before if w else x * following)
                rows = slice(u * eighth, (u + 1) * eighth)
                far_rows = slice(half + u * eighth, half + (u + 1) * eighth)
                for t in (2 * i, 2 * i + 1):
                    own = slice(t * feat, (t + 1) * feat)
                    near = forced[rows, own] + fine[:eighth]
                    far = forced[far_rows, own] + fine[eighth:]
                    folded[0, rows, own] = (near + far).astype(jnp.bfloat16)
                    folded[1, rows, own] = (near - far).astype(jnp.bfloat16)
                if u % 2 == 1:
                    size = eighth
                    collect(after, next_cols, (2 * i + u // 2) * size, size)
                    yield

    def transform(_, slot):
        folded = slot[0]
        for parity in range(2):
            for at in range(0, lanes, 2 * feat):
                start = parity * lanes + at
                out[:, start : start + 2 * feat] = jnp.dot(
                    table[parity],
                    folded[parity, :, at : at + 2 * feat],
                    preferred_element_type=jnp.float32,
                ).astype(jnp.bfloat16)
                yield

    @pl.when(step == 0)
    def _():
        wide[...] = answers[...].astype(jnp.float32)
        collect(0, held[1], 0, count)

    staggered(
        step,
        steps,
        fold,
        transform,
        ((held[0], held[1], held[3]), (held[2], held[3], held[1])),
    )


def to_waves(slots, table, forced, answers):
    lanes = forced.shape[1]
    slot_total, feat = answers.shape
    depth = table.shape[1]
    lats = lanes // feat
    together = lats_together(lats)
    own = together * feat
    count = together // 2 * (NLON // 4)
    steps = lats // together
    slot = [
        pltpu.VMEM((2, NLON // 2, own), jnp.bfloat16),
        pltpu.VMEM((count, feat), jnp.float32),
    ]
    return pl.pallas_call(
        functools.partial(to_waves_kernel, steps),
        grid_spec=pltpu.PrefetchScalarGridSpec(
            num_scalar_prefetch=1,
            grid=(steps + 1,),
            in_specs=[
                pl.BlockSpec((2, depth, NLON // 2), lambda i, s: (0, 0, 0)),
                pl.BlockSpec((NLON, own), lambda i, s: (0, jnp.minimum(i, steps - 1))),
                pl.BlockSpec((slot_total, feat), lambda i, s: (0, 0)),
            ],
            out_specs=pl.BlockSpec((depth, 2 * own), lambda i, s: (0, jnp.maximum(i - 1, 0))),
            scratch_shapes=[
                pltpu.VMEM((slot_total, feat), jnp.float32),
                *slot,
                *slot,
            ],
        ),
        out_shape=jax.ShapeDtypeStruct((depth, 2 * lanes), jnp.bfloat16),
        compiler_params=params(),
        name="to_waves",
    )(slots, table, forced, answers)


def forward_legendre_kernel(steps, low, coeffs, leg, merge, out, *slots):
    step = pl.program_id(0)
    group, degrees, channels = out.shape
    feat = channels // 2
    lat_total = leg.shape[2]
    devices, rows = coeffs.shape[:2]
    lats = lat_total // devices
    pitch = lat_total + PITCH_EXTRA
    middle = (degrees - 1) // 2

    def turn(_, held):
        for d in range(devices):
            for a in range(lats):
                for parity in range(2):
                    start = parity * rows * pitch + d * lats + a
                    lane = lane_start(a, parity, lats, feat)
                    held[pl.ds(start, rows, stride=pitch), :] = coeffs[
                        d, :, lane : lane + feat
                    ].astype(jnp.float32)
            if (d + 1) % (devices // 4) == 0:
                yield

    def transform(number, held):
        for g in range(group):
            own_low = low[number * group + g]
            lower = degrees - 1 - own_low
            sides = []
            for s in range(2):
                parity = (own_low + s) % 2
                parts = []
                for r in range(2):
                    start = (parity * rows + 2 * g + r) * pitch
                    parts.append(held[pl.ds(pl.multiple_of(start, 8), lat_total), :])
                sides.append(jnp.concatenate(parts, axis=1).astype(jnp.bfloat16))
            first = jnp.dot(leg[g], sides[0], preferred_element_type=jnp.float32)
            second = jnp.dot(leg[g, middle:], sides[1], preferred_element_type=jnp.float32)
            on_first = lax.broadcasted_iota(jnp.int32, second.shape, 0) < lower - middle
            chosen = jnp.concatenate(
                [first[:middle], jnp.where(on_first, first[middle:], second)], axis=0
            )
            out[g] = jnp.dot(
                chosen.astype(jnp.bfloat16), merge[...], preferred_element_type=jnp.float32
            ).astype(jnp.bfloat16)
            yield

    staggered(step, steps, turn, transform, slots)


def forward_legendre(coeffs, legendre, local_low, channels):
    devices, rows, lanes = coeffs.shape
    pairs, degrees, lat_total = legendre.shape
    group = group_of(pairs)
    steps = pairs // group
    slot = pltpu.VMEM((4 * group * (lat_total + PITCH_EXTRA), channels // 2), jnp.float32)
    return pl.pallas_call(
        functools.partial(forward_legendre_kernel, steps),
        grid=(steps + 1,),
        in_specs=[
            pl.BlockSpec(memory_space=pltpu.SMEM),
            pl.BlockSpec(
                (devices, 2 * group, lanes), lambda i: (0, jnp.minimum(i, steps - 1), 0)
            ),
            pl.BlockSpec((group, degrees, lat_total), lambda i: (jnp.maximum(i - 1, 0), 0, 0)),
            pl.BlockSpec((channels, channels), lambda i: (0, 0)),
        ],
        out_specs=pl.BlockSpec((group, degrees, channels), lambda i: (jnp.maximum(i - 1, 0), 0, 0)),
        out_shape=jax.ShapeDtypeStruct((pairs, degrees, channels), jnp.bfloat16),
        scratch_shapes=[slot, slot],
        compiler_params=params(),
        name="forward_legendre",
    )(local_low, coeffs, legendre, split_matrix(channels).T)


def exchange(blocks):
    return lax.all_to_all(blocks, "wave", split_axis=0, concat_axis=0, tiled=True)


def on_device(spectral, legendre, pair_low, routes, w_in, w_mid, w_out):
    pairs, degrees, channels = spectral.shape
    feat = channels // 2
    devices = lax.axis_size("wave")
    local_low = lax.dynamic_slice_in_dim(pair_low, lax.axis_index("wave") * pairs, pairs)

    sent = inverse_legendre(spectral, jnp.swapaxes(legendre, 1, 2), local_low, devices)
    arrived = exchange(sent)
    inverse_table, forward_table = zonal_tables(pair_low, degrees - 1)
    regimes = routes[:, 0]
    capacity = 2 * regimes.shape[0] // devices
    slots = regimes * capacity + slot_positions(regimes, devices)

    forced, outgoing = to_grid(
        slots, inverse_table, arrived.reshape(-1, arrived.shape[2]), devices * capacity, feat
    )
    columns = exchange(outgoing.reshape(devices, capacity, feat))
    answers = network(columns.reshape(-1, feat), w_in[0], w_mid[0], w_out[0])
    incoming = exchange(answers.reshape(devices, capacity, feat)).reshape(-1, feat)
    waves = to_waves(slots, forward_table, forced, incoming)
    received = exchange(waves.reshape(arrived.shape))
    return forward_legendre(received, legendre, local_low, channels)


def solution(mesh):
    placed = (
        P(("grp", "wave"), None, None),
        P("wave", None, None),
        P(),
        P(("grp", "wave"), None),
        P("wave", None, None),
        P("wave", None, None),
        P("wave", None, None),
    )
    return jax.shard_map(
        on_device,
        mesh=mesh,
        in_specs=placed,
        out_specs=P(("grp", "wave"), None, None),
        check_vma=False,
    )
```

```python
import functools
import itertools
import math

import jax
import jax.numpy as jnp
import numpy as np
from jax import lax
from jax.experimental import pallas as pl
from jax.experimental.pallas import tpu as pltpu
from jax.sharding import PartitionSpec as P

NLON = 1280
FIELDS = 4
SPREAD = ((0.375, 0.625, 0.0), (0.125, 0.875, 0.0), (0.0, 0.875, 0.125), (0.0, 0.625, 0.375))
PITCH_EXTRA = 8


def params(mebibytes):
    return pltpu.CompilerParams(vmem_limit_bytes=mebibytes * 1024 * 1024)


def in_hbm(array):
    return pltpu.with_memory_space_constraint(array, pltpu.HBM)


def slot_positions(regimes, experts_total):
    onehot = (regimes[:, None] == jnp.arange(experts_total, dtype=jnp.int32)).astype(jnp.int32)
    ranking = jnp.cumsum(onehot, axis=0) - 1
    return jnp.sum(ranking * onehot, axis=1)


def zonal_tables(pair_low, wave_total):
    other = wave_total - 1 - pair_low
    even = jnp.where(pair_low % 2 == 0, pair_low, other)
    waves = jnp.stack([even, wave_total - 1 - even]).reshape(2, -1, 1)
    quarter = jnp.array([0, NLON // 4], jnp.int32).reshape(1, 1, 2)
    rows = (2, waves.shape[1], 2)
    waves_k = jnp.broadcast_to(waves, rows).reshape(2, -1)
    turn_k = jnp.broadcast_to(quarter, rows).reshape(2, -1)
    order = jnp.arange(NLON // 2, dtype=jnp.int32)
    longitude = 4 * (order % (NLON // 8)) + order // (NLON // 8)

    def cosines(wave, turn, lon):
        phases = (wave * lon + turn) % NLON
        return jnp.cos(phases.astype(jnp.float32) * jnp.float32(2.0 * math.pi / NLON))

    scale = jnp.where(waves_k == 0, jnp.float32(1.0), jnp.float32(2.0))
    inverse = scale[:, None, :] * cosines(
        waves_k[:, None, :], turn_k[:, None, :], longitude[None, :, None]
    )
    forward = jnp.float32(1.0 / math.sqrt(NLON)) * cosines(
        waves_k[:, :, None], turn_k[:, :, None], longitude[None, None, :]
    )
    return inverse.astype(jnp.bfloat16), forward.astype(jnp.bfloat16)


def lats_together(lats):
    return 4 if lats % 4 == 0 else 2


def lane_start(lat, parity, lats, feat):
    together = lats_together(lats)
    return ((lat // together * 2 + parity) * together + lat % together) * feat


def split_matrix(width):
    channel = np.arange(width)
    target = (channel % 2) * (width // 2) + channel // 2
    return (target[:, None] == channel[None, :]).astype(jnp.bfloat16)


def group_of(pairs):
    return 4 if pairs % 4 == 0 else pairs


def staggered(step, steps, first, second, slots):
    def run(*parts):
        for _ in itertools.zip_longest(*parts):
            pass

    @pl.when(step == 0)
    def _():
        run(first(0, slots[0]))

    for odd in range(2):

        @pl.when((step > 0) & (step < steps) & (step % 2 == odd))
        def _(odd=odd):
            run(second(step - 1, slots[1 - odd]), first(step, slots[odd]))

    @pl.when(step == steps)
    def _():
        run(second(steps - 1, slots[(steps - 1) % 2]))


def inverse_legendre_kernel(steps, low, spec, leg, split, out, *slots):
    step = pl.program_id(0)
    group, degrees, channels = spec.shape
    feat = channels // 2
    lat_total = leg.shape[1]
    devices, rows = out.shape[:2]
    lats = lat_total // devices
    pitch = lat_total + PITCH_EXTRA
    middle = (degrees - 1) // 2
    skip = middle // 256 * 256

    first_pair = lax.axis_index("wave") * steps * group

    def transform(number, held):
        for g in range(group):
            own_low = low[first_pair + number * group + g]
            lower = degrees - 1 - own_low
            coeffs = jnp.dot(spec[g], split[...], preferred_element_type=jnp.float32)
            tail = coeffs[middle:]
            on_first = lax.broadcasted_iota(jnp.int32, tail.shape, 0) < lower - middle
            first = jnp.concatenate([coeffs[:middle], jnp.where(on_first, tail, 0.0)], axis=0)
            second = jnp.concatenate(
                [jnp.zeros((middle - skip, channels), jnp.float32), jnp.where(on_first, 0.0, tail)],
                axis=0,
            )
            sides = (
                jnp.dot(leg[g], first.astype(jnp.bfloat16), preferred_element_type=jnp.float32),
                jnp.dot(
                    leg[g, :, skip:],
                    second.astype(jnp.bfloat16),
                    preferred_element_type=jnp.float32,
                ),
            )
            for s in range(2):
                parity = (own_low + s) % 2
                for r in range(2):
                    start = (parity * rows + 2 * g + r) * pitch
                    held[pl.ds(pl.multiple_of(start, 8), lat_total), :] = sides[s][
                        :, r * feat : (r + 1) * feat
                    ]
            yield

    def turn(_, held):
        for d in range(devices):
            for a in range(lats):
                for parity in range(2):
                    start = parity * rows * pitch + d * lats + a
                    own = held[pl.ds(start, rows, stride=pitch), :]
                    lane = lane_start(a, parity, lats, feat)
                    out[d, :, lane : lane + feat] = own.astype(jnp.bfloat16)
            if (d + 1) % (devices // 4) == 0:
                yield

    staggered(step, steps, transform, turn, slots)


def inverse_legendre(spectral, legendre, pair_low, devices):
    pairs, degrees, channels = spectral.shape
    lat_total = legendre.shape[1]
    lanes = lat_total // devices * channels
    group = group_of(pairs)
    steps = pairs // group
    slot = pltpu.VMEM((4 * group * (lat_total + PITCH_EXTRA), channels // 2), jnp.float32)
    return pl.pallas_call(
        functools.partial(inverse_legendre_kernel, steps),
        grid=(steps + 1,),
        in_specs=[
            pl.BlockSpec(memory_space=pltpu.SMEM),
            pl.BlockSpec((group, degrees, channels), lambda i: (jnp.minimum(i, steps - 1), 0, 0)),
            pl.BlockSpec((group, lat_total, degrees), lambda i: (jnp.minimum(i, steps - 1), 0, 0)),
            pl.BlockSpec((channels, channels), lambda i: (0, 0)),
        ],
        out_specs=pl.BlockSpec(
            (devices, 2 * group, lanes), lambda i: (0, jnp.maximum(i - 1, 0), 0)
        ),
        out_shape=pltpu.HBM((devices, 2 * pairs, lanes), jnp.bfloat16),
        scratch_shapes=[slot, slot],
        compiler_params=params(56),
        name="inverse_legendre",
    )(pair_low, in_hbm(spectral), in_hbm(legendre), split_matrix(channels))


def to_grid_kernel(steps, slots, table, coeffs, forced, packed, cols, sent, *held):
    step = pl.program_id(0)
    count, feat = cols.shape
    lanes = forced.shape[1]
    half = table.shape[1]
    eighth = half // 4
    lat_rows = lanes // (2 * feat)

    def transform(_, parts):
        for parity in range(2):
            for at in range(0, lanes, 2 * feat):
                start = parity * lanes + at
                parts[parity, :, at : at + 2 * feat] = jnp.dot(
                    table[parity],
                    coeffs[:, start : start + 2 * feat],
                    preferred_element_type=jnp.float32,
                )
                yield

    def finish(number, parts):
        for i in range(lat_rows):
            totals = [jnp.zeros((eighth, feat), jnp.float32) for _ in range(2)]
            for t in (2 * i, 2 * i + 1):
                own = slice(t * feat, (t + 1) * feat)
                for u in range(4):
                    rows = slice(u * eighth, (u + 1) * eighth)
                    even, odd = parts[0, rows, own], parts[1, rows, own]
                    for h, field in enumerate((even + odd, even - odd)):
                        totals[h] = totals[h] + field
                        start = h * half + u * eighth
                        product = field * pltpu.roll(field, feat - feat // FIELDS, axis=1)
                        forced[start : start + eighth, own] = product.astype(jnp.bfloat16)
                if t == 2 * i:
                    yield
            for h in range(2):
                start = (2 * i + h) * eighth
                cols[start : start + eighth, :] = (
                    (totals[h] * 0.125).astype(jnp.bfloat16).astype(jnp.float32)
                )
            for k in range(2 * i * eighth, 2 * (i + 1) * eighth):
                sent[pl.ds(slots[number * count + k], 1), :] = cols[pl.ds(k, 1), :]
            yield

    @pl.when(step == 0)
    def _():
        sent[...] = jnp.zeros_like(sent)

    staggered(step, steps, transform, finish, held)

    @pl.when(step == steps)
    def _():
        packed[...] = sent[...].astype(jnp.bfloat16)


def to_grid(slots, table, coeffs, slot_total, feat):
    depth, lanes = coeffs.shape
    lats = lanes // (2 * feat)
    together = lats_together(lats)
    own = together * feat
    count = together // 2 * (NLON // 4)
    steps = lats // together
    part = pltpu.VMEM((2, NLON // 2, own), jnp.float32)
    return pl.pallas_call(
        functools.partial(to_grid_kernel, steps),
        grid_spec=pltpu.PrefetchScalarGridSpec(
            num_scalar_prefetch=1,
            grid=(steps + 1,),
            in_specs=[
                pl.BlockSpec((2, NLON // 2, depth), lambda i, s: (0, 0, 0)),
                pl.BlockSpec((depth, 2 * own), lambda i, s: (0, jnp.minimum(i, steps - 1))),
            ],
            out_specs=[
                pl.BlockSpec((NLON, own), lambda i, s: (0, jnp.maximum(i - 1, 0))),
                pl.BlockSpec((slot_total, feat), lambda i, s: (0, 0)),
            ],
            scratch_shapes=[
                pltpu.VMEM((count, feat), jnp.float32),
                pltpu.VMEM((slot_total, feat), jnp.float32),
                part,
                part,
            ],
        ),
        out_shape=[
            pltpu.HBM((NLON, lats * feat), jnp.bfloat16),
            jax.ShapeDtypeStruct((slot_total, feat), jnp.bfloat16),
        ],
        compiler_params=params(36),
        name="to_grid",
    )(slots, table, in_hbm(coeffs))


def silu(v):
    return 0.5 * v * (1.0 + jnp.tanh(0.5 * v))


def network_kernel(cols, weight_in, weight_mid, weight_out, out):
    rows = out.shape[0] // 2
    for half in range(2):
        own = slice(half * rows, (half + 1) * rows)
        hidden = jnp.dot(cols[own], weight_in[...], preferred_element_type=jnp.float32)
        hidden = silu(hidden).astype(jnp.bfloat16)
        deeper = jnp.dot(hidden, weight_mid[...], preferred_element_type=jnp.float32)
        deeper = silu(deeper).astype(jnp.bfloat16)
        result = jnp.dot(deeper, weight_out[...], preferred_element_type=jnp.float32)
        out[own] = result.astype(jnp.bfloat16)


def network(columns, weight_in, weight_mid, weight_out):
    rows, feat = columns.shape
    hid = weight_in.shape[1]
    block = rows // 8
    return pl.pallas_call(
        network_kernel,
        grid=(rows // block,),
        in_specs=[
            pl.BlockSpec((block, feat), lambda i: (i, 0)),
            pl.BlockSpec((feat, hid), lambda i: (0, 0)),
            pl.BlockSpec((hid, hid), lambda i: (0, 0)),
            pl.BlockSpec((hid, feat), lambda i: (0, 0)),
        ],
        out_specs=pl.BlockSpec((block, feat), lambda i: (i, 0)),
        out_shape=jax.ShapeDtypeStruct((rows, feat), jnp.bfloat16),
        compiler_params=params(36),
        name="network",
    )(columns, weight_in, weight_mid, weight_out)


def to_waves_kernel(steps, slots, table, forced, answers, out, wide, *held):
    step = pl.program_id(0)
    count, feat = held[1].shape
    lanes = forced.shape[1]
    half = table.shape[2]
    eighth = half // 4
    quarter = 2 * eighth

    def collect(number, cols, start, size):
        for k in range(start, start + size):
            cols[pl.ds(k, 1), :] = wide[pl.ds(slots[number * count + k], 1), :]

    def fold(number, slot):
        folded, cols, next_cols = slot
        after = jnp.minimum(number + 1, steps - 1)
        for i in range(count // quarter):
            coarse = cols[i * quarter : (i + 1) * quarter, :]
            before = pltpu.roll(coarse, 1, axis=0)
            following = pltpu.roll(coarse, quarter - 1, axis=0)
            for u in range(4):
                w, v, x = SPREAD[u]
                fine = v * coarse + (w * before if w else x * following)
                rows = slice(u * eighth, (u + 1) * eighth)
                far_rows = slice(half + u * eighth, half + (u + 1) * eighth)
                for t in (2 * i, 2 * i + 1):
                    own = slice(t * feat, (t + 1) * feat)
                    near = forced[rows, own] + fine[:eighth]
                    far = forced[far_rows, own] + fine[eighth:]
                    folded[0, rows, own] = (near + far).astype(jnp.bfloat16)
                    folded[1, rows, own] = (near - far).astype(jnp.bfloat16)
                if u % 2 == 1:
                    size = eighth
                    collect(after, next_cols, (2 * i + u // 2) * size, size)
                    yield

    def transform(_, slot):
        folded = slot[0]
        for parity in range(2):
            for at in range(0, lanes, 2 * feat):
                start = parity * lanes + at
                out[:, start : start + 2 * feat] = jnp.dot(
                    table[parity],
                    folded[parity, :, at : at + 2 * feat],
                    preferred_element_type=jnp.float32,
                ).astype(jnp.bfloat16)
                yield

    @pl.when(step == 0)
    def _():
        wide[...] = answers[...].astype(jnp.float32)
        collect(0, held[1], 0, count)

    staggered(
        step,
        steps,
        fold,
        transform,
        ((held[0], held[1], held[3]), (held[2], held[3], held[1])),
    )


def to_waves(slots, table, forced, answers):
    lanes = forced.shape[1]
    slot_total, feat = answers.shape
    depth = table.shape[1]
    lats = lanes // feat
    together = lats_together(lats)
    own = together * feat
    count = together // 2 * (NLON // 4)
    steps = lats // together
    slot = [
        pltpu.VMEM((2, NLON // 2, own), jnp.bfloat16),
        pltpu.VMEM((count, feat), jnp.float32),
    ]
    return pl.pallas_call(
        functools.partial(to_waves_kernel, steps),
        grid_spec=pltpu.PrefetchScalarGridSpec(
            num_scalar_prefetch=1,
            grid=(steps + 1,),
            in_specs=[
                pl.BlockSpec((2, depth, NLON // 2), lambda i, s: (0, 0, 0)),
                pl.BlockSpec((NLON, own), lambda i, s: (0, jnp.minimum(i, steps - 1))),
                pl.BlockSpec((slot_total, feat), lambda i, s: (0, 0)),
            ],
            out_specs=pl.BlockSpec((depth, 2 * own), lambda i, s: (0, jnp.maximum(i - 1, 0))),
            scratch_shapes=[
                pltpu.VMEM((slot_total, feat), jnp.float32),
                *slot,
                *slot,
            ],
        ),
        out_shape=pltpu.HBM((depth, 2 * lanes), jnp.bfloat16),
        compiler_params=params(36),
        name="to_waves",
    )(slots, table, in_hbm(forced), answers)


def forward_legendre_kernel(steps, low, coeffs, leg, merge, out, *slots):
    step = pl.program_id(0)
    group, degrees, channels = out.shape
    feat = channels // 2
    lat_total = leg.shape[2]
    devices, rows = coeffs.shape[:2]
    lats = lat_total // devices
    pitch = lat_total + PITCH_EXTRA
    middle = (degrees - 1) // 2

    def turn(_, held):
        for d in range(devices):
            for a in range(lats):
                for parity in range(2):
                    start = parity * rows * pitch + d * lats + a
                    lane = lane_start(a, parity, lats, feat)
                    held[pl.ds(start, rows, stride=pitch), :] = coeffs[
                        d, :, lane : lane + feat
                    ].astype(jnp.float32)
            if (d + 1) % (devices // 4) == 0:
                yield

    first_pair = lax.axis_index("wave") * steps * group

    def transform(number, held):
        for g in range(group):
            own_low = low[first_pair + number * group + g]
            lower = degrees - 1 - own_low
            sides = []
            for s in range(2):
                parity = (own_low + s) % 2
                parts = []
                for r in range(2):
                    start = (parity * rows + 2 * g + r) * pitch
                    parts.append(held[pl.ds(pl.multiple_of(start, 8), lat_total), :])
                sides.append(jnp.concatenate(parts, axis=1).astype(jnp.bfloat16))
            first = jnp.dot(leg[g], sides[0], preferred_element_type=jnp.float32)
            second = jnp.dot(leg[g, middle:], sides[1], preferred_element_type=jnp.float32)
            on_first = lax.broadcasted_iota(jnp.int32, second.shape, 0) < lower - middle
            chosen = jnp.concatenate(
                [first[:middle], jnp.where(on_first, first[middle:], second)], axis=0
            )
            out[g] = jnp.dot(
                chosen.astype(jnp.bfloat16), merge[...], preferred_element_type=jnp.float32
            ).astype(jnp.bfloat16)
            yield

    staggered(step, steps, turn, transform, slots)


def forward_legendre(coeffs, legendre, pair_low, channels):
    devices, rows, lanes = coeffs.shape
    pairs, degrees, lat_total = legendre.shape
    group = group_of(pairs)
    steps = pairs // group
    slot = pltpu.VMEM((4 * group * (lat_total + PITCH_EXTRA), channels // 2), jnp.float32)
    return pl.pallas_call(
        functools.partial(forward_legendre_kernel, steps),
        grid=(steps + 1,),
        in_specs=[
            pl.BlockSpec(memory_space=pltpu.SMEM),
            pl.BlockSpec(
                (devices, 2 * group, lanes), lambda i: (0, jnp.minimum(i, steps - 1), 0)
            ),
            pl.BlockSpec((group, degrees, lat_total), lambda i: (jnp.maximum(i - 1, 0), 0, 0)),
            pl.BlockSpec((channels, channels), lambda i: (0, 0)),
        ],
        out_specs=pl.BlockSpec((group, degrees, channels), lambda i: (jnp.maximum(i - 1, 0), 0, 0)),
        out_shape=jax.ShapeDtypeStruct((pairs, degrees, channels), jnp.bfloat16),
        scratch_shapes=[slot, slot],
        compiler_params=params(56),
        name="forward_legendre",
    )(pair_low, in_hbm(coeffs), in_hbm(legendre), split_matrix(channels).T)


def exchange(blocks):
    return lax.all_to_all(blocks, "wave", split_axis=0, concat_axis=0, tiled=True)


def on_device(spectral, legendre, pair_low, routes, w_in, w_mid, w_out):
    _, degrees, channels = spectral.shape
    feat = channels // 2
    devices = lax.axis_size("wave")
    sent = inverse_legendre(spectral, jnp.swapaxes(legendre, 1, 2), pair_low, devices)
    arrived = exchange(sent)
    inverse_table, forward_table = zonal_tables(pair_low, degrees - 1)
    regimes = routes[:, 0]
    capacity = 2 * regimes.shape[0] // devices
    slots = regimes * capacity + slot_positions(regimes, devices)

    forced, outgoing = to_grid(
        slots, inverse_table, arrived.reshape(-1, arrived.shape[2]), devices * capacity, feat
    )
    columns = exchange(outgoing.reshape(devices, capacity, feat))
    answers = network(columns.reshape(-1, feat), w_in[0], w_mid[0], w_out[0])
    incoming = exchange(answers.reshape(devices, capacity, feat)).reshape(-1, feat)
    waves = to_waves(slots, forward_table, forced, incoming)
    received = exchange(waves.reshape(arrived.shape))
    return forward_legendre(received, legendre, pair_low, channels)


def solution(mesh):
    placed = (
        P(("grp", "wave"), None, None),
        P("wave", None, None),
        P(),
        P(("grp", "wave"), None),
        P("wave", None, None),
        P("wave", None, None),
        P("wave", None, None),
    )
    return jax.shard_map(
        on_device,
        mesh=mesh,
        in_specs=placed,
        out_specs=P(("grp", "wave"), None, None),
        check_vma=False,
    )
```

```python
import functools
import itertools
import math

import jax
import jax.numpy as jnp
import numpy as np
from jax import lax
from jax.experimental import pallas as pl
from jax.experimental.pallas import tpu as pltpu
from jax.sharding import PartitionSpec as P

NLON = 1280
FIELDS = 4
SPREAD = ((0.375, 0.625, 0.0), (0.125, 0.875, 0.0), (0.0, 0.875, 0.125), (0.0, 0.625, 0.375))
PITCH_EXTRA = 8


def params(mebibytes):
    return pltpu.CompilerParams(vmem_limit_bytes=mebibytes * 1024 * 1024)


def in_hbm(array):
    return pltpu.with_memory_space_constraint(array, pltpu.HBM)


def slot_positions(regimes, experts_total):
    onehot = (regimes[:, None] == jnp.arange(experts_total, dtype=jnp.int32)).astype(jnp.int32)
    ranking = jnp.cumsum(onehot, axis=0) - 1
    return jnp.sum(ranking * onehot, axis=1)


def zonal_tables(pair_low, wave_total):
    other = wave_total - 1 - pair_low
    even = jnp.where(pair_low % 2 == 0, pair_low, other)
    waves = jnp.stack([even, wave_total - 1 - even]).reshape(2, -1, 1)
    quarter = jnp.array([0, NLON // 4], jnp.int32).reshape(1, 1, 2)
    rows = (2, waves.shape[1], 2)
    waves_k = jnp.broadcast_to(waves, rows).reshape(2, -1)
    turn_k = jnp.broadcast_to(quarter, rows).reshape(2, -1)
    order = jnp.arange(NLON // 2, dtype=jnp.int32)
    longitude = 4 * (order % (NLON // 8)) + order // (NLON // 8)

    def cosines(wave, turn, lon):
        phases = (wave * lon + turn) % NLON
        return jnp.cos(phases.astype(jnp.float32) * jnp.float32(2.0 * math.pi / NLON))

    scale = jnp.where(waves_k == 0, jnp.float32(1.0), jnp.float32(2.0))
    inverse = scale[:, None, :] * cosines(
        waves_k[:, None, :], turn_k[:, None, :], longitude[None, :, None]
    )
    forward = jnp.float32(1.0 / math.sqrt(NLON)) * cosines(
        waves_k[:, :, None], turn_k[:, :, None], longitude[None, None, :]
    )
    return inverse.astype(jnp.bfloat16), forward.astype(jnp.bfloat16)


def lats_together(lats):
    return 4 if lats % 4 == 0 else 2


def lane_start(lat, parity, lats, feat):
    together = lats_together(lats)
    return ((lat // together * 2 + parity) * together + lat % together) * feat


def split_matrix(width):
    channel = np.arange(width)
    target = (channel % 2) * (width // 2) + channel // 2
    return (target[:, None] == channel[None, :]).astype(jnp.bfloat16)


def group_of(pairs):
    return 4 if pairs % 4 == 0 else pairs


def staggered(step, steps, first, second, slots):
    def run(*parts):
        for _ in itertools.zip_longest(*parts):
            pass

    @pl.when(step == 0)
    def _():
        run(first(0, slots[0]))

    for odd in range(2):

        @pl.when((step > 0) & (step < steps) & (step % 2 == odd))
        def _(odd=odd):
            run(second(step - 1, slots[1 - odd]), first(step, slots[odd]))

    @pl.when(step == steps)
    def _():
        run(second(steps - 1, slots[(steps - 1) % 2]))


def inverse_legendre_kernel(steps, low, spec, leg, split, out, *slots):
    step = pl.program_id(0)
    group, degrees, channels = spec.shape
    feat = channels // 2
    lat_total = leg.shape[1]
    devices, rows = out.shape[:2]
    lats = lat_total // devices
    pitch = lat_total + PITCH_EXTRA
    middle = (degrees - 1) // 2
    skip = middle // 256 * 256

    first_pair = lax.axis_index("wave") * steps * group

    def prepare(number, g):
        own_low = low[first_pair + number * group + g]
        lower = degrees - 1 - own_low
        coeffs = jnp.dot(spec[g], split[...], preferred_element_type=jnp.float32)
        tail = coeffs[middle:]
        on_first = lax.broadcasted_iota(jnp.int32, tail.shape, 0) < lower - middle
        first = jnp.concatenate([coeffs[:middle], jnp.where(on_first, tail, 0.0)], axis=0)
        second = jnp.concatenate(
            [jnp.zeros((middle - skip, channels), jnp.float32), jnp.where(on_first, 0.0, tail)],
            axis=0,
        )
        return own_low, first.astype(jnp.bfloat16), second.astype(jnp.bfloat16)

    def transform(number, held):
        ready = prepare(number, 0)
        for g in range(group):
            own_low, first, second = ready
            if g + 1 < group:
                ready = prepare(number, g + 1)
            sides = (
                jnp.dot(leg[g], first, preferred_element_type=jnp.float32),
                jnp.dot(leg[g, :, skip:], second, preferred_element_type=jnp.float32),
            )
            for s in range(2):
                parity = (own_low + s) % 2
                for r in range(2):
                    start = (parity * rows + 2 * g + r) * pitch
                    held[pl.ds(pl.multiple_of(start, 8), lat_total), :] = sides[s][
                        :, r * feat : (r + 1) * feat
                    ]
            yield

    def turn(_, held):
        for d in range(devices):
            for a in range(lats):
                for parity in range(2):
                    start = parity * rows * pitch + d * lats + a
                    own = held[pl.ds(start, rows, stride=pitch), :]
                    lane = lane_start(a, parity, lats, feat)
                    out[d, :, lane : lane + feat] = own.astype(jnp.bfloat16)
            if (d + 1) % (devices // 4) == 0:
                yield

    staggered(step, steps, transform, turn, slots)


def inverse_legendre(spectral, legendre, pair_low, devices):
    pairs, degrees, channels = spectral.shape
    lat_total = legendre.shape[1]
    lanes = lat_total // devices * channels
    group = group_of(pairs)
    steps = pairs // group
    slot = pltpu.VMEM((4 * group * (lat_total + PITCH_EXTRA), channels // 2), jnp.float32)
    return pl.pallas_call(
        functools.partial(inverse_legendre_kernel, steps),
        grid=(steps + 1,),
        in_specs=[
            pl.BlockSpec(memory_space=pltpu.SMEM),
            pl.BlockSpec((group, degrees, channels), lambda i: (jnp.minimum(i, steps - 1), 0, 0)),
            pl.BlockSpec((group, lat_total, degrees), lambda i: (jnp.minimum(i, steps - 1), 0, 0)),
            pl.BlockSpec((channels, channels), lambda i: (0, 0)),
        ],
        out_specs=pl.BlockSpec(
            (devices, 2 * group, lanes), lambda i: (0, jnp.maximum(i - 1, 0), 0)
        ),
        out_shape=pltpu.HBM((devices, 2 * pairs, lanes), jnp.bfloat16),
        scratch_shapes=[slot, slot],
        compiler_params=params(56),
        name="inverse_legendre",
    )(pair_low, in_hbm(spectral), in_hbm(legendre), split_matrix(channels))


def to_grid_kernel(steps, slots, table, coeffs, forced, packed, cols, sent, *held):
    step = pl.program_id(0)
    count, feat = cols.shape
    lanes = forced.shape[1]
    half = table.shape[1]
    eighth = half // 4
    lat_rows = lanes // (2 * feat)

    def transform(_, parts):
        for parity in range(2):
            for at in range(0, lanes, 2 * feat):
                start = parity * lanes + at
                parts[parity, :, at : at + 2 * feat] = jnp.dot(
                    table[parity],
                    coeffs[:, start : start + 2 * feat],
                    preferred_element_type=jnp.float32,
                )
                yield

    def finish(number, parts):
        for i in range(lat_rows):
            totals = [jnp.zeros((eighth, feat), jnp.float32) for _ in range(2)]
            for t in (2 * i, 2 * i + 1):
                own = slice(t * feat, (t + 1) * feat)
                for u in range(4):
                    rows = slice(u * eighth, (u + 1) * eighth)
                    even, odd = parts[0, rows, own], parts[1, rows, own]
                    for h, field in enumerate((even + odd, even - odd)):
                        totals[h] = totals[h] + field
                        start = h * half + u * eighth
                        product = field * pltpu.roll(field, feat - feat // FIELDS, axis=1)
                        forced[start : start + eighth, own] = product.astype(jnp.bfloat16)
                if t == 2 * i:
                    yield
            for h in range(2):
                start = (2 * i + h) * eighth
                cols[start : start + eighth, :] = (
                    (totals[h] * 0.125).astype(jnp.bfloat16).astype(jnp.float32)
                )
            for k in range(2 * i * eighth, 2 * (i + 1) * eighth):
                sent[pl.ds(slots[number * count + k], 1), :] = cols[pl.ds(k, 1), :]
            yield

    @pl.when(step == 0)
    def _():
        sent[...] = jnp.zeros_like(sent)

    staggered(step, steps, transform, finish, held)

    @pl.when(step == steps)
    def _():
        packed[...] = sent[...].astype(jnp.bfloat16)


def to_grid(slots, table, coeffs, slot_total, feat):
    depth, lanes = coeffs.shape
    lats = lanes // (2 * feat)
    together = lats_together(lats)
    own = together * feat
    count = together // 2 * (NLON // 4)
    steps = lats // together
    part = pltpu.VMEM((2, NLON // 2, own), jnp.float32)
    return pl.pallas_call(
        functools.partial(to_grid_kernel, steps),
        grid_spec=pltpu.PrefetchScalarGridSpec(
            num_scalar_prefetch=1,
            grid=(steps + 1,),
            in_specs=[
                pl.BlockSpec((2, NLON // 2, depth), lambda i, s: (0, 0, 0)),
                pl.BlockSpec((depth, 2 * own), lambda i, s: (0, jnp.minimum(i, steps - 1))),
            ],
            out_specs=[
                pl.BlockSpec((NLON, own), lambda i, s: (0, jnp.maximum(i - 1, 0))),
                pl.BlockSpec((slot_total, feat), lambda i, s: (0, 0)),
            ],
            scratch_shapes=[
                pltpu.VMEM((count, feat), jnp.float32),
                pltpu.VMEM((slot_total, feat), jnp.float32),
                part,
                part,
            ],
        ),
        out_shape=[
            pltpu.HBM((NLON, lats * feat), jnp.bfloat16),
            jax.ShapeDtypeStruct((slot_total, feat), jnp.bfloat16),
        ],
        compiler_params=params(36),
        name="to_grid",
    )(slots, table, in_hbm(coeffs))


def silu(v):
    return 0.5 * v * (1.0 + jnp.tanh(0.5 * v))


def network_kernel(cols, weight_in, weight_mid, weight_out, out):
    parts = 2
    rows = out.shape[0] // parts

    def enter(part):
        hidden = jnp.dot(
            cols[part * rows : (part + 1) * rows],
            weight_in[...],
            preferred_element_type=jnp.float32,
        )
        return silu(hidden).astype(jnp.bfloat16)

    def leave(part, deeper):
        result = jnp.dot(deeper, weight_out[...], preferred_element_type=jnp.float32)
        out[part * rows : (part + 1) * rows] = result.astype(jnp.bfloat16)

    hidden, deeper = enter(0), None
    for part in range(parts):
        current = hidden
        if part + 1 < parts:
            hidden = enter(part + 1)
        middle = jnp.dot(current, weight_mid[...], preferred_element_type=jnp.float32)
        if deeper is not None:
            leave(part - 1, deeper)
        deeper = silu(middle).astype(jnp.bfloat16)
    leave(parts - 1, deeper)


def network(columns, weight_in, weight_mid, weight_out):
    rows, feat = columns.shape
    hid = weight_in.shape[1]
    block = rows // 4
    return pl.pallas_call(
        network_kernel,
        grid=(rows // block,),
        in_specs=[
            pl.BlockSpec((block, feat), lambda i: (i, 0)),
            pl.BlockSpec((feat, hid), lambda i: (0, 0)),
            pl.BlockSpec((hid, hid), lambda i: (0, 0)),
            pl.BlockSpec((hid, feat), lambda i: (0, 0)),
        ],
        out_specs=pl.BlockSpec((block, feat), lambda i: (i, 0)),
        out_shape=jax.ShapeDtypeStruct((rows, feat), jnp.bfloat16),
        compiler_params=params(36),
        name="network",
    )(columns, weight_in, weight_mid, weight_out)


def to_waves_kernel(steps, slots, table, forced, answers, out, wide, *held):
    step = pl.program_id(0)
    count, feat = held[1].shape
    lanes = forced.shape[1]
    half = table.shape[2]
    eighth = half // 4
    quarter = 2 * eighth

    def collect(number, cols, start, size):
        for k in range(start, start + size):
            cols[pl.ds(k, 1), :] = wide[pl.ds(slots[number * count + k], 1), :]

    def fold(number, slot):
        folded, cols, next_cols = slot
        after = jnp.minimum(number + 1, steps - 1)
        for i in range(count // quarter):
            coarse = cols[i * quarter : (i + 1) * quarter, :]
            before = pltpu.roll(coarse, 1, axis=0)
            following = pltpu.roll(coarse, quarter - 1, axis=0)
            for u in range(4):
                w, v, x = SPREAD[u]
                fine = v * coarse + (w * before if w else x * following)
                rows = slice(u * eighth, (u + 1) * eighth)
                far_rows = slice(half + u * eighth, half + (u + 1) * eighth)
                for t in (2 * i, 2 * i + 1):
                    own = slice(t * feat, (t + 1) * feat)
                    near = forced[rows, own] + fine[:eighth]
                    far = forced[far_rows, own] + fine[eighth:]
                    folded[0, rows, own] = (near + far).astype(jnp.bfloat16)
                    folded[1, rows, own] = (near - far).astype(jnp.bfloat16)
                if u % 2 == 1:
                    size = eighth
                    collect(after, next_cols, (2 * i + u // 2) * size, size)
                    yield

    def transform(_, slot):
        folded = slot[0]
        for parity in range(2):
            for at in range(0, lanes, 2 * feat):
                start = parity * lanes + at
                out[:, start : start + 2 * feat] = jnp.dot(
                    table[parity],
                    folded[parity, :, at : at + 2 * feat],
                    preferred_element_type=jnp.float32,
                ).astype(jnp.bfloat16)
                yield

    @pl.when(step == 0)
    def _():
        wide[...] = answers[...].astype(jnp.float32)
        collect(0, held[1], 0, count)

    staggered(
        step,
        steps,
        fold,
        transform,
        ((held[0], held[1], held[3]), (held[2], held[3], held[1])),
    )


def to_waves(slots, table, forced, answers):
    lanes = forced.shape[1]
    slot_total, feat = answers.shape
    depth = table.shape[1]
    lats = lanes // feat
    together = lats_together(lats)
    own = together * feat
    count = together // 2 * (NLON // 4)
    steps = lats // together
    slot = [
        pltpu.VMEM((2, NLON // 2, own), jnp.bfloat16),
        pltpu.VMEM((count, feat), jnp.float32),
    ]
    return pl.pallas_call(
        functools.partial(to_waves_kernel, steps),
        grid_spec=pltpu.PrefetchScalarGridSpec(
            num_scalar_prefetch=1,
            grid=(steps + 1,),
            in_specs=[
                pl.BlockSpec((2, depth, NLON // 2), lambda i, s: (0, 0, 0)),
                pl.BlockSpec((NLON, own), lambda i, s: (0, jnp.minimum(i, steps - 1))),
                pl.BlockSpec((slot_total, feat), lambda i, s: (0, 0)),
            ],
            out_specs=pl.BlockSpec((depth, 2 * own), lambda i, s: (0, jnp.maximum(i - 1, 0))),
            scratch_shapes=[
                pltpu.VMEM((slot_total, feat), jnp.float32),
                *slot,
                *slot,
            ],
        ),
        out_shape=pltpu.HBM((depth, 2 * lanes), jnp.bfloat16),
        compiler_params=params(36),
        name="to_waves",
    )(slots, table, in_hbm(forced), answers)


def forward_legendre_kernel(steps, low, coeffs, leg, merge, out, *slots):
    step = pl.program_id(0)
    group, degrees, channels = out.shape
    feat = channels // 2
    lat_total = leg.shape[2]
    devices, rows = coeffs.shape[:2]
    lats = lat_total // devices
    pitch = lat_total + PITCH_EXTRA
    middle = (degrees - 1) // 2

    def turn(_, held):
        for d in range(devices):
            for a in range(lats):
                for parity in range(2):
                    start = parity * rows * pitch + d * lats + a
                    lane = lane_start(a, parity, lats, feat)
                    held[pl.ds(start, rows, stride=pitch), :] = coeffs[
                        d, :, lane : lane + feat
                    ].astype(jnp.float32)
            if (d + 1) % (devices // 4) == 0:
                yield

    first_pair = lax.axis_index("wave") * steps * group

    def transform(number, held):
        waiting = None
        for g in range(group):
            own_low = low[first_pair + number * group + g]
            lower = degrees - 1 - own_low
            sides = []
            for s in range(2):
                parity = (own_low + s) % 2
                parts = []
                for r in range(2):
                    start = (parity * rows + 2 * g + r) * pitch
                    parts.append(held[pl.ds(pl.multiple_of(start, 8), lat_total), :])
                sides.append(jnp.concatenate(parts, axis=1).astype(jnp.bfloat16))
            first = jnp.dot(leg[g], sides[0], preferred_element_type=jnp.float32)
            second = jnp.dot(leg[g, middle:], sides[1], preferred_element_type=jnp.float32)
            if waiting is not None:
                finish(g - 1, waiting)
            on_first = lax.broadcasted_iota(jnp.int32, second.shape, 0) < lower - middle
            chosen = jnp.concatenate(
                [first[:middle], jnp.where(on_first, first[middle:], second)], axis=0
            )
            waiting = chosen.astype(jnp.bfloat16)
            yield
        finish(group - 1, waiting)

    def finish(g, chosen):
        out[g] = jnp.dot(chosen, merge[...], preferred_element_type=jnp.float32).astype(
            jnp.bfloat16
        )

    staggered(step, steps, turn, transform, slots)


def forward_legendre(coeffs, legendre, pair_low, channels):
    devices, rows, lanes = coeffs.shape
    pairs, degrees, lat_total = legendre.shape
    group = group_of(pairs)
    steps = pairs // group
    slot = pltpu.VMEM((4 * group * (lat_total + PITCH_EXTRA), channels // 2), jnp.float32)
    return pl.pallas_call(
        functools.partial(forward_legendre_kernel, steps),
        grid=(steps + 1,),
        in_specs=[
            pl.BlockSpec(memory_space=pltpu.SMEM),
            pl.BlockSpec(
                (devices, 2 * group, lanes), lambda i: (0, jnp.minimum(i, steps - 1), 0)
            ),
            pl.BlockSpec((group, degrees, lat_total), lambda i: (jnp.maximum(i - 1, 0), 0, 0)),
            pl.BlockSpec((channels, channels), lambda i: (0, 0)),
        ],
        out_specs=pl.BlockSpec((group, degrees, channels), lambda i: (jnp.maximum(i - 1, 0), 0, 0)),
        out_shape=jax.ShapeDtypeStruct((pairs, degrees, channels), jnp.bfloat16),
        scratch_shapes=[slot, slot],
        compiler_params=params(56),
        name="forward_legendre",
    )(pair_low, in_hbm(coeffs), in_hbm(legendre), split_matrix(channels).T)


def exchange(blocks):
    return lax.all_to_all(blocks, "wave", split_axis=0, concat_axis=0, tiled=True)


def on_device(spectral, legendre, pair_low, routes, w_in, w_mid, w_out):
    _, degrees, channels = spectral.shape
    feat = channels // 2
    devices = lax.axis_size("wave")
    sent = inverse_legendre(spectral, jnp.swapaxes(legendre, 1, 2), pair_low, devices)
    arrived = exchange(sent)
    inverse_table, forward_table = zonal_tables(pair_low, degrees - 1)
    regimes = routes[:, 0]
    capacity = 2 * regimes.shape[0] // devices
    slots = regimes * capacity + slot_positions(regimes, devices)

    forced, outgoing = to_grid(
        slots, inverse_table, arrived.reshape(-1, arrived.shape[2]), devices * capacity, feat
    )
    columns = exchange(outgoing.reshape(devices, capacity, feat))
    answers = network(columns.reshape(-1, feat), w_in[0], w_mid[0], w_out[0])
    incoming = exchange(answers.reshape(devices, capacity, feat)).reshape(-1, feat)
    waves = to_waves(slots, forward_table, forced, incoming)
    received = exchange(waves.reshape(arrived.shape))
    return forward_legendre(received, legendre, pair_low, channels)


def solution(mesh):
    placed = (
        P(("grp", "wave"), None, None),
        P("wave", None, None),
        P(),
        P(("grp", "wave"), None),
        P("wave", None, None),
        P("wave", None, None),
        P("wave", None, None),
    )
    return jax.shard_map(
        on_device,
        mesh=mesh,
        in_specs=placed,
        out_specs=P(("grp", "wave"), None, None),
        check_vma=False,
    )
```

```python
import functools
import itertools
import math

import jax
import jax.numpy as jnp
import numpy as np
from jax import lax
from jax.experimental import pallas as pl
from jax.experimental.pallas import tpu as pltpu
from jax.sharding import PartitionSpec as P

NLON = 1280
FIELDS = 4
SPREAD = ((0.375, 0.625, 0.0), (0.125, 0.875, 0.0), (0.0, 0.875, 0.125), (0.0, 0.625, 0.375))
PITCH_EXTRA = 8


def params(mebibytes):
    return pltpu.CompilerParams(vmem_limit_bytes=mebibytes * 1024 * 1024)


def in_hbm(array):
    return pltpu.with_memory_space_constraint(array, pltpu.HBM)


def slot_positions(regimes, experts_total):
    onehot = (regimes[:, None] == jnp.arange(experts_total, dtype=jnp.int32)).astype(jnp.int32)
    ranking = jnp.cumsum(onehot, axis=0) - 1
    return jnp.sum(ranking * onehot, axis=1)


def zonal_tables(pair_low, wave_total):
    other = wave_total - 1 - pair_low
    even = jnp.where(pair_low % 2 == 0, pair_low, other)
    waves = jnp.stack([even, wave_total - 1 - even]).reshape(2, -1, 1)
    quarter = jnp.array([0, NLON // 4], jnp.int32).reshape(1, 1, 2)
    rows = (2, waves.shape[1], 2)
    waves_k = jnp.broadcast_to(waves, rows).reshape(2, -1)
    turn_k = jnp.broadcast_to(quarter, rows).reshape(2, -1)
    order = jnp.arange(NLON // 2, dtype=jnp.int32)
    longitude = 4 * (order % (NLON // 8)) + order // (NLON // 8)

    def cosines(wave, turn, lon):
        phases = (wave * lon + turn) % NLON
        return jnp.cos(phases.astype(jnp.float32) * jnp.float32(2.0 * math.pi / NLON))

    scale = jnp.where(waves_k == 0, jnp.float32(1.0), jnp.float32(2.0))
    inverse = scale[:, None, :] * cosines(
        waves_k[:, None, :], turn_k[:, None, :], longitude[None, :, None]
    )
    forward = jnp.float32(1.0 / math.sqrt(NLON)) * cosines(
        waves_k[:, :, None], turn_k[:, :, None], longitude[None, None, :]
    )
    return inverse.astype(jnp.bfloat16), forward.astype(jnp.bfloat16)


def lats_together(lats):
    return 4 if lats % 4 == 0 else 2


def lane_start(lat, parity, lats, feat):
    together = lats_together(lats)
    return ((lat // together * 2 + parity) * together + lat % together) * feat


def split_matrix(width):
    channel = np.arange(width)
    target = (channel % 2) * (width // 2) + channel // 2
    return (target[:, None] == channel[None, :]).astype(jnp.bfloat16)


def group_of(pairs):
    return 4 if pairs % 4 == 0 else pairs


def staggered(step, steps, first, second, slots):
    def run(*parts):
        for _ in itertools.zip_longest(*parts):
            pass

    @pl.when(step == 0)
    def _():
        run(first(0, slots[0]))

    for odd in range(2):

        @pl.when((step > 0) & (step < steps) & (step % 2 == odd))
        def _(odd=odd):
            run(second(step - 1, slots[1 - odd]), first(step, slots[odd]))

    @pl.when(step == steps)
    def _():
        run(second(steps - 1, slots[(steps - 1) % 2]))


def inverse_legendre_kernel(steps, low, spec, leg, split, out, *slots):
    step = pl.program_id(0)
    group, degrees, channels = spec.shape
    feat = channels // 2
    lat_total = leg.shape[1]
    devices, rows = out.shape[:2]
    lats = lat_total // devices
    pitch = lat_total + PITCH_EXTRA
    middle = (degrees - 1) // 2
    skip = middle // 256 * 256

    first_pair = lax.axis_index("wave") * steps * group

    def prepare(number, g):
        own_low = low[first_pair + number * group + g]
        lower = degrees - 1 - own_low
        coeffs = jnp.dot(spec[g], split[...], preferred_element_type=jnp.float32)
        tail = coeffs[middle:]
        on_first = lax.broadcasted_iota(jnp.int32, tail.shape, 0) < lower - middle
        first = jnp.concatenate([coeffs[:middle], jnp.where(on_first, tail, 0.0)], axis=0)
        second = jnp.concatenate(
            [jnp.zeros((middle - skip, channels), jnp.float32), jnp.where(on_first, 0.0, tail)],
            axis=0,
        )
        return own_low, first.astype(jnp.bfloat16), second.astype(jnp.bfloat16)

    def transform(number, held):
        ready = prepare(number, 0)
        for g in range(group):
            own_low, first, second = ready
            if g + 1 < group:
                ready = prepare(number, g + 1)
            sides = (
                jnp.dot(leg[g], first, preferred_element_type=jnp.float32),
                jnp.dot(leg[g, :, skip:], second, preferred_element_type=jnp.float32),
            )
            for s in range(2):
                parity = (own_low + s) % 2
                for r in range(2):
                    start = (parity * rows + 2 * g + r) * pitch
                    held[pl.ds(pl.multiple_of(start, 8), lat_total), :] = sides[s][
                        :, r * feat : (r + 1) * feat
                    ]
            yield

    def turn(_, held):
        for d in range(devices):
            for a in range(lats):
                for parity in range(2):
                    start = parity * rows * pitch + d * lats + a
                    own = held[pl.ds(start, rows, stride=pitch), :]
                    lane = lane_start(a, parity, lats, feat)
                    out[d, :, lane : lane + feat] = own.astype(jnp.bfloat16)
            if (d + 1) % (devices // 4) == 0:
                yield

    staggered(step, steps, transform, turn, slots)


def inverse_legendre(spectral, legendre, pair_low, devices):
    pairs, degrees, channels = spectral.shape
    lat_total = legendre.shape[1]
    lanes = lat_total // devices * channels
    group = group_of(pairs)
    steps = pairs // group
    slot = pltpu.VMEM(((4 * group + 1) * (lat_total + PITCH_EXTRA), channels // 2), jnp.float32)
    return pl.pallas_call(
        functools.partial(inverse_legendre_kernel, steps),
        grid=(steps + 1,),
        in_specs=[
            pl.BlockSpec(memory_space=pltpu.SMEM),
            pl.BlockSpec((group, degrees, channels), lambda i: (jnp.minimum(i, steps - 1), 0, 0)),
            pl.BlockSpec((group, lat_total, degrees), lambda i: (jnp.minimum(i, steps - 1), 0, 0)),
            pl.BlockSpec((channels, channels), lambda i: (0, 0)),
        ],
        out_specs=pl.BlockSpec(
            (devices, 2 * group, lanes), lambda i: (0, jnp.maximum(i - 1, 0), 0)
        ),
        out_shape=pltpu.HBM((devices, 2 * pairs, lanes), jnp.bfloat16),
        scratch_shapes=[slot, slot],
        compiler_params=params(56),
        name="inverse_legendre",
    )(pair_low, in_hbm(spectral), in_hbm(legendre), split_matrix(channels))


def to_grid_kernel(steps, slots, table, coeffs, forced, packed, cols, sent, *held):
    step = pl.program_id(0)
    count, feat = cols.shape
    lanes = forced.shape[1]
    half = table.shape[1]
    eighth = half // 4
    lat_rows = lanes // (2 * feat)

    def transform(_, parts):
        for parity in range(2):
            for at in range(0, lanes, 2 * feat):
                start = parity * lanes + at
                parts[parity, :, at : at + 2 * feat] = jnp.dot(
                    table[parity],
                    coeffs[:, start : start + 2 * feat],
                    preferred_element_type=jnp.float32,
                )
                yield

    def finish(number, parts):
        for i in range(lat_rows):
            totals = [jnp.zeros((eighth, feat), jnp.float32) for _ in range(2)]
            for t in (2 * i, 2 * i + 1):
                own = slice(t * feat, (t + 1) * feat)
                for u in range(4):
                    rows = slice(u * eighth, (u + 1) * eighth)
                    even, odd = parts[0, rows, own], parts[1, rows, own]
                    for h, field in enumerate((even + odd, even - odd)):
                        totals[h] = totals[h] + field
                        start = h * half + u * eighth
                        product = field * pltpu.roll(field, feat - feat // FIELDS, axis=1)
                        forced[start : start + eighth, own] = product.astype(jnp.bfloat16)
                if t == 2 * i:
                    yield
            for h in range(2):
                start = (2 * i + h) * eighth
                cols[start : start + eighth, :] = (
                    (totals[h] * 0.125).astype(jnp.bfloat16).astype(jnp.float32)
                )
            for k in range(2 * i * eighth, 2 * (i + 1) * eighth):
                sent[pl.ds(slots[number * count + k], 1), :] = cols[pl.ds(k, 1), :]
            yield

    @pl.when(step == 0)
    def _():
        sent[...] = jnp.zeros_like(sent)

    staggered(step, steps, transform, finish, held)

    @pl.when(step == steps)
    def _():
        packed[...] = sent[...].astype(jnp.bfloat16)


def to_grid(slots, table, coeffs, slot_total, feat):
    depth, lanes = coeffs.shape
    lats = lanes // (2 * feat)
    together = lats_together(lats)
    own = together * feat
    count = together // 2 * (NLON // 4)
    steps = lats // together
    part = pltpu.VMEM((2, NLON // 2, own), jnp.float32)
    return pl.pallas_call(
        functools.partial(to_grid_kernel, steps),
        grid_spec=pltpu.PrefetchScalarGridSpec(
            num_scalar_prefetch=1,
            grid=(steps + 1,),
            in_specs=[
                pl.BlockSpec((2, NLON // 2, depth), lambda i, s: (0, 0, 0)),
                pl.BlockSpec((depth, 2 * own), lambda i, s: (0, jnp.minimum(i, steps - 1))),
            ],
            out_specs=[
                pl.BlockSpec((NLON, own), lambda i, s: (0, jnp.maximum(i - 1, 0))),
                pl.BlockSpec((slot_total, feat), lambda i, s: (0, 0)),
            ],
            scratch_shapes=[
                pltpu.VMEM((count, feat), jnp.float32),
                pltpu.VMEM((slot_total, feat), jnp.float32),
                part,
                part,
            ],
        ),
        out_shape=[
            pltpu.HBM((NLON, lats * feat), jnp.bfloat16),
            jax.ShapeDtypeStruct((slot_total, feat), jnp.bfloat16),
        ],
        compiler_params=params(36),
        name="to_grid",
    )(slots, table, in_hbm(coeffs))


def silu(v):
    return 0.5 * v * (1.0 + jnp.tanh(0.5 * v))


def network_kernel(cols, weight_in, weight_mid, weight_out, out):
    parts = 2
    rows = out.shape[0] // parts

    def enter(part):
        hidden = jnp.dot(
            cols[part * rows : (part + 1) * rows],
            weight_in[...],
            preferred_element_type=jnp.float32,
        )
        return silu(hidden).astype(jnp.bfloat16)

    def leave(part, deeper):
        result = jnp.dot(deeper, weight_out[...], preferred_element_type=jnp.float32)
        out[part * rows : (part + 1) * rows] = result.astype(jnp.bfloat16)

    hidden, deeper = enter(0), None
    for part in range(parts):
        current = hidden
        if part + 1 < parts:
            hidden = enter(part + 1)
        middle = jnp.dot(current, weight_mid[...], preferred_element_type=jnp.float32)
        if deeper is not None:
            leave(part - 1, deeper)
        deeper = silu(middle).astype(jnp.bfloat16)
    leave(parts - 1, deeper)


def network(columns, weight_in, weight_mid, weight_out):
    rows, feat = columns.shape
    hid = weight_in.shape[1]
    block = rows // 4
    return pl.pallas_call(
        network_kernel,
        grid=(rows // block,),
        in_specs=[
            pl.BlockSpec((block, feat), lambda i: (i, 0)),
            pl.BlockSpec((feat, hid), lambda i: (0, 0)),
            pl.BlockSpec((hid, hid), lambda i: (0, 0)),
            pl.BlockSpec((hid, feat), lambda i: (0, 0)),
        ],
        out_specs=pl.BlockSpec((block, feat), lambda i: (i, 0)),
        out_shape=jax.ShapeDtypeStruct((rows, feat), jnp.bfloat16),
        compiler_params=params(36),
        name="network",
    )(columns, weight_in, weight_mid, weight_out)


def to_waves_kernel(steps, slots, table, forced, answers, out, wide, *held):
    step = pl.program_id(0)
    count, feat = held[1].shape
    lanes = forced.shape[1]
    half = table.shape[2]
    eighth = half // 4
    quarter = 2 * eighth

    def collect(number, cols, start, size):
        for k in range(start, start + size):
            cols[pl.ds(k, 1), :] = wide[pl.ds(slots[number * count + k], 1), :]

    def fold(number, slot):
        folded, cols, next_cols = slot
        after = jnp.minimum(number + 1, steps - 1)
        for i in range(count // quarter):
            coarse = cols[i * quarter : (i + 1) * quarter, :]
            before = pltpu.roll(coarse, 1, axis=0)
            following = pltpu.roll(coarse, quarter - 1, axis=0)
            for u in range(4):
                w, v, x = SPREAD[u]
                fine = v * coarse + (w * before if w else x * following)
                rows = slice(u * eighth, (u + 1) * eighth)
                far_rows = slice(half + u * eighth, half + (u + 1) * eighth)
                for t in (2 * i, 2 * i + 1):
                    own = slice(t * feat, (t + 1) * feat)
                    near = forced[rows, own] + fine[:eighth]
                    far = forced[far_rows, own] + fine[eighth:]
                    folded[0, rows, own] = (near + far).astype(jnp.bfloat16)
                    folded[1, rows, own] = (near - far).astype(jnp.bfloat16)
                if u % 2 == 1:
                    size = eighth
                    collect(after, next_cols, (2 * i + u // 2) * size, size)
                    yield

    def transform(_, slot):
        folded = slot[0]
        for parity in range(2):
            for at in range(0, lanes, 2 * feat):
                start = parity * lanes + at
                out[:, start : start + 2 * feat] = jnp.dot(
                    table[parity],
                    folded[parity, :, at : at + 2 * feat],
                    preferred_element_type=jnp.float32,
                ).astype(jnp.bfloat16)
                yield

    @pl.when(step == 0)
    def _():
        wide[...] = answers[...].astype(jnp.float32)
        collect(0, held[1], 0, count)

    staggered(
        step,
        steps,
        fold,
        transform,
        ((held[0], held[1], held[3]), (held[2], held[3], held[1])),
    )


def to_waves(slots, table, forced, answers):
    lanes = forced.shape[1]
    slot_total, feat = answers.shape
    depth = table.shape[1]
    lats = lanes // feat
    together = lats_together(lats)
    own = together * feat
    count = together // 2 * (NLON // 4)
    steps = lats // together
    slot = [
        pltpu.VMEM((2, NLON // 2, own), jnp.bfloat16),
        pltpu.VMEM((count, feat), jnp.float32),
    ]
    return pl.pallas_call(
        functools.partial(to_waves_kernel, steps),
        grid_spec=pltpu.PrefetchScalarGridSpec(
            num_scalar_prefetch=1,
            grid=(steps + 1,),
            in_specs=[
                pl.BlockSpec((2, depth, NLON // 2), lambda i, s: (0, 0, 0)),
                pl.BlockSpec((NLON, own), lambda i, s: (0, jnp.minimum(i, steps - 1))),
                pl.BlockSpec((slot_total, feat), lambda i, s: (0, 0)),
            ],
            out_specs=pl.BlockSpec((depth, 2 * own), lambda i, s: (0, jnp.maximum(i - 1, 0))),
            scratch_shapes=[
                pltpu.VMEM((slot_total, feat), jnp.float32),
                *slot,
                *slot,
            ],
        ),
        out_shape=pltpu.HBM((depth, 2 * lanes), jnp.bfloat16),
        compiler_params=params(36),
        name="to_waves",
    )(slots, table, in_hbm(forced), answers)


def forward_legendre_kernel(steps, low, coeffs, leg, merge, out, *slots):
    step = pl.program_id(0)
    group, degrees, channels = out.shape
    feat = channels // 2
    lat_total = leg.shape[2]
    devices, rows = coeffs.shape[:2]
    lats = lat_total // devices
    pitch = lat_total + PITCH_EXTRA
    middle = (degrees - 1) // 2

    def turn(_, held):
        for d in range(devices):
            for a in range(lats):
                for parity in range(2):
                    start = parity * rows * pitch + d * lats + a
                    lane = lane_start(a, parity, lats, feat)
                    held[pl.ds(start, rows, stride=pitch), :] = coeffs[
                        d, :, lane : lane + feat
                    ].astype(jnp.float32)
            if (d + 1) % (devices // 4) == 0:
                yield

    first_pair = lax.axis_index("wave") * steps * group

    def transform(number, held):
        waiting = None
        for g in range(group):
            own_low = low[first_pair + number * group + g]
            lower = degrees - 1 - own_low
            sides = []
            for s in range(2):
                parity = (own_low + s) % 2
                parts = []
                for r in range(2):
                    start = (parity * rows + 2 * g + r) * pitch
                    parts.append(held[pl.ds(pl.multiple_of(start, 8), lat_total), :])
                sides.append(jnp.concatenate(parts, axis=1).astype(jnp.bfloat16))
            first = jnp.dot(leg[g], sides[0], preferred_element_type=jnp.float32)
            second = jnp.dot(leg[g, middle:], sides[1], preferred_element_type=jnp.float32)
            if waiting is not None:
                finish(g - 1, waiting)
            on_first = lax.broadcasted_iota(jnp.int32, second.shape, 0) < lower - middle
            chosen = jnp.concatenate(
                [first[:middle], jnp.where(on_first, first[middle:], second)], axis=0
            )
            waiting = chosen.astype(jnp.bfloat16)
            yield
        finish(group - 1, waiting)

    def finish(g, chosen):
        out[g] = jnp.dot(chosen, merge[...], preferred_element_type=jnp.float32).astype(
            jnp.bfloat16
        )

    staggered(step, steps, turn, transform, slots)


def forward_legendre(coeffs, legendre, pair_low, channels):
    devices, rows, lanes = coeffs.shape
    pairs, degrees, lat_total = legendre.shape
    group = group_of(pairs)
    steps = pairs // group
    slot = pltpu.VMEM(((4 * group + 1) * (lat_total + PITCH_EXTRA), channels // 2), jnp.float32)
    return pl.pallas_call(
        functools.partial(forward_legendre_kernel, steps),
        grid=(steps + 1,),
        in_specs=[
            pl.BlockSpec(memory_space=pltpu.SMEM),
            pl.BlockSpec(
                (devices, 2 * group, lanes), lambda i: (0, jnp.minimum(i, steps - 1), 0)
            ),
            pl.BlockSpec((group, degrees, lat_total), lambda i: (jnp.maximum(i - 1, 0), 0, 0)),
            pl.BlockSpec((channels, channels), lambda i: (0, 0)),
        ],
        out_specs=pl.BlockSpec((group, degrees, channels), lambda i: (jnp.maximum(i - 1, 0), 0, 0)),
        out_shape=jax.ShapeDtypeStruct((pairs, degrees, channels), jnp.bfloat16),
        scratch_shapes=[slot, slot],
        compiler_params=params(56),
        name="forward_legendre",
    )(pair_low, in_hbm(coeffs), in_hbm(legendre), split_matrix(channels).T)


def exchange(blocks):
    return lax.all_to_all(blocks, "wave", split_axis=0, concat_axis=0, tiled=True)


def on_device(spectral, legendre, pair_low, routes, w_in, w_mid, w_out):
    _, degrees, channels = spectral.shape
    feat = channels // 2
    devices = lax.axis_size("wave")
    sent = inverse_legendre(spectral, jnp.swapaxes(legendre, 1, 2), pair_low, devices)
    arrived = exchange(sent)
    inverse_table, forward_table = zonal_tables(pair_low, degrees - 1)
    regimes = routes[:, 0]
    capacity = 2 * regimes.shape[0] // devices
    slots = regimes * capacity + slot_positions(regimes, devices)

    forced, outgoing = to_grid(
        slots, inverse_table, arrived.reshape(-1, arrived.shape[2]), devices * capacity, feat
    )
    columns = exchange(outgoing.reshape(devices, capacity, feat))
    answers = network(columns.reshape(-1, feat), w_in[0], w_mid[0], w_out[0])
    incoming = exchange(answers.reshape(devices, capacity, feat)).reshape(-1, feat)
    waves = to_waves(slots, forward_table, forced, incoming)
    received = exchange(waves.reshape(arrived.shape))
    return forward_legendre(received, legendre, pair_low, channels)


def solution(mesh):
    placed = (
        P(("grp", "wave"), None, None),
        P("wave", None, None),
        P(),
        P(("grp", "wave"), None),
        P("wave", None, None),
        P("wave", None, None),
        P("wave", None, None),
    )
    return jax.shard_map(
        on_device,
        mesh=mesh,
        in_specs=placed,
        out_specs=P(("grp", "wave"), None, None),
        check_vma=False,
    )
```

```python
import functools
import itertools
import math

import jax
import jax.numpy as jnp
import numpy as np
from jax import lax
from jax.experimental import pallas as pl
from jax.experimental.pallas import tpu as pltpu
from jax.sharding import PartitionSpec as P

NLON = 1280
FIELDS = 4
SPREAD = ((0.375, 0.625, 0.0), (0.125, 0.875, 0.0), (0.0, 0.875, 0.125), (0.0, 0.625, 0.375))
PITCH_EXTRA = 8


def params(mebibytes):
    return pltpu.CompilerParams(vmem_limit_bytes=mebibytes * 1024 * 1024)


WHOLE = pl.BlockSpec(memory_space=pltpu.VMEM)


def in_hbm(array):
    return pltpu.with_memory_space_constraint(array, pltpu.HBM)


def slot_positions(regimes, experts_total):
    onehot = (regimes[:, None] == jnp.arange(experts_total, dtype=jnp.int32)).astype(jnp.int32)
    ranking = jnp.cumsum(onehot, axis=0) - 1
    return jnp.sum(ranking * onehot, axis=1)


def zonal_tables(pair_low, wave_total):
    other = wave_total - 1 - pair_low
    even = jnp.where(pair_low % 2 == 0, pair_low, other)
    waves = jnp.stack([even, wave_total - 1 - even]).reshape(2, -1, 1)
    quarter = jnp.array([0, NLON // 4], jnp.int32).reshape(1, 1, 2)
    rows = (2, waves.shape[1], 2)
    waves_k = jnp.broadcast_to(waves, rows).reshape(2, -1)
    turn_k = jnp.broadcast_to(quarter, rows).reshape(2, -1)
    order = jnp.arange(NLON // 2, dtype=jnp.int32)
    longitude = 4 * (order % (NLON // 8)) + order // (NLON // 8)

    def cosines(wave, turn, lon):
        phases = (wave * lon + turn) % NLON
        return jnp.cos(phases.astype(jnp.float32) * jnp.float32(2.0 * math.pi / NLON))

    scale = jnp.where(waves_k == 0, jnp.float32(1.0), jnp.float32(2.0))
    inverse = scale[:, None, :] * cosines(
        waves_k[:, None, :], turn_k[:, None, :], longitude[None, :, None]
    )
    forward = jnp.float32(1.0 / math.sqrt(NLON)) * cosines(
        waves_k[:, :, None], turn_k[:, :, None], longitude[None, None, :]
    )
    return inverse.astype(jnp.bfloat16), forward.astype(jnp.bfloat16)


def lats_together(lats):
    return 4 if lats % 4 == 0 else 2


def lane_start(lat, parity, lats, feat):
    together = lats_together(lats)
    return ((lat // together * 2 + parity) * together + lat % together) * feat


def split_matrix(width):
    channel = np.arange(width)
    target = (channel % 2) * (width // 2) + channel // 2
    return (target[:, None] == channel[None, :]).astype(jnp.bfloat16)


def group_of(pairs):
    return 4 if pairs % 4 == 0 else pairs


def staggered(step, steps, first, second, slots):
    def run(*parts):
        for _ in itertools.zip_longest(*parts):
            pass

    @pl.when(step == 0)
    def _():
        run(first(0, slots[0]))

    for odd in range(2):

        @pl.when((step > 0) & (step < steps) & (step % 2 == odd))
        def _(odd=odd):
            run(second(step - 1, slots[1 - odd]), first(step, slots[odd]))

    @pl.when(step == steps)
    def _():
        run(second(steps - 1, slots[(steps - 1) % 2]))


def inverse_legendre_kernel(steps, low, spec, leg, split, out, *slots):
    step = pl.program_id(0)
    group, degrees, channels = spec.shape
    feat = channels // 2
    lat_total = leg.shape[1]
    devices, rows = out.shape[:2]
    lats = lat_total // devices
    pitch = lat_total + PITCH_EXTRA
    middle = (degrees - 1) // 2
    skip = middle // 256 * 256

    first_pair = lax.axis_index("wave") * steps * group

    def prepare(number, g):
        own_low = low[first_pair + number * group + g]
        lower = degrees - 1 - own_low
        coeffs = jnp.dot(spec[g], split[...], preferred_element_type=jnp.float32)
        tail = coeffs[middle:]
        on_first = lax.broadcasted_iota(jnp.int32, tail.shape, 0) < lower - middle
        first = jnp.concatenate([coeffs[:middle], jnp.where(on_first, tail, 0.0)], axis=0)
        second = jnp.concatenate(
            [jnp.zeros((middle - skip, channels), jnp.float32), jnp.where(on_first, 0.0, tail)],
            axis=0,
        )
        return own_low, first.astype(jnp.bfloat16), second.astype(jnp.bfloat16)

    def transform(number, held):
        ready = prepare(number, 0)
        for g in range(group):
            own_low, first, second = ready
            if g + 1 < group:
                ready = prepare(number, g + 1)
            sides = (
                jnp.dot(leg[g], first, preferred_element_type=jnp.float32),
                jnp.dot(leg[g, :, skip:], second, preferred_element_type=jnp.float32),
            )
            for s in range(2):
                parity = (own_low + s) % 2
                for r in range(2):
                    start = (parity * rows + 2 * g + r) * pitch
                    held[pl.ds(pl.multiple_of(start, 8), lat_total), :] = sides[s][
                        :, r * feat : (r + 1) * feat
                    ]
            yield

    def turn(_, held):
        for d in range(devices):
            for a in range(lats):
                for parity in range(2):
                    start = parity * rows * pitch + d * lats + a
                    own = held[pl.ds(start, rows, stride=pitch), :]
                    lane = lane_start(a, parity, lats, feat)
                    out[d, :, lane : lane + feat] = own.astype(jnp.bfloat16)
            if (d + 1) % (devices // 4) == 0:
                yield

    staggered(step, steps, transform, turn, slots)


def inverse_legendre(spectral, legendre, pair_low, devices):
    pairs, degrees, channels = spectral.shape
    lat_total = legendre.shape[1]
    lanes = lat_total // devices * channels
    group = group_of(pairs)
    steps = pairs // group
    slot = pltpu.VMEM(((4 * group + 1) * (lat_total + PITCH_EXTRA), channels // 2), jnp.float32)
    return pl.pallas_call(
        functools.partial(inverse_legendre_kernel, steps),
        grid=(steps + 1,),
        in_specs=[
            pl.BlockSpec(memory_space=pltpu.SMEM),
            pl.BlockSpec((group, degrees, channels), lambda i: (jnp.minimum(i, steps - 1), 0, 0)),
            pl.BlockSpec((group, lat_total, degrees), lambda i: (jnp.minimum(i, steps - 1), 0, 0)),
            pl.BlockSpec((channels, channels), lambda i: (0, 0)),
        ],
        out_specs=pl.BlockSpec(
            (devices, 2 * group, lanes), lambda i: (0, jnp.maximum(i - 1, 0), 0)
        ),
        out_shape=pltpu.HBM((devices, 2 * pairs, lanes), jnp.bfloat16),
        scratch_shapes=[slot, slot],
        compiler_params=params(56),
        name="inverse_legendre",
    )(pair_low, in_hbm(spectral), in_hbm(legendre), split_matrix(channels))


def to_grid_kernel(steps, slots, table, coeffs, forced, packed, cols, sent, *held):
    step = pl.program_id(0)
    count, feat = cols.shape
    lanes = forced.shape[1]
    half = table.shape[1]
    eighth = half // 4
    lat_rows = lanes // (2 * feat)

    def transform(_, parts):
        for parity in range(2):
            for at in range(0, lanes, 2 * feat):
                start = parity * lanes + at
                parts[parity, :, at : at + 2 * feat] = jnp.dot(
                    table[parity],
                    coeffs[:, start : start + 2 * feat],
                    preferred_element_type=jnp.float32,
                )
                yield

    def finish(number, parts):
        for i in range(lat_rows):
            totals = [jnp.zeros((eighth, feat), jnp.float32) for _ in range(2)]
            for t in (2 * i, 2 * i + 1):
                own = slice(t * feat, (t + 1) * feat)
                for u in range(4):
                    rows = slice(u * eighth, (u + 1) * eighth)
                    even, odd = parts[0, rows, own], parts[1, rows, own]
                    for h, field in enumerate((even + odd, even - odd)):
                        totals[h] = totals[h] + field
                        start = h * half + u * eighth
                        product = field * pltpu.roll(field, feat - feat // FIELDS, axis=1)
                        forced[start : start + eighth, own] = product.astype(jnp.bfloat16)
                if t == 2 * i:
                    yield
            for h in range(2):
                start = (2 * i + h) * eighth
                cols[start : start + eighth, :] = (
                    (totals[h] * 0.125).astype(jnp.bfloat16).astype(jnp.float32)
                )
            for k in range(2 * i * eighth, 2 * (i + 1) * eighth):
                sent[pl.ds(slots[number * count + k], 1), :] = cols[pl.ds(k, 1), :]
            yield

    @pl.when(step == 0)
    def _():
        sent[...] = jnp.zeros_like(sent)

    staggered(step, steps, transform, finish, held)

    @pl.when(step == steps)
    def _():
        packed[...] = sent[...].astype(jnp.bfloat16)


def to_grid(slots, table, coeffs, slot_total, feat):
    depth, lanes = coeffs.shape
    lats = lanes // (2 * feat)
    together = lats_together(lats)
    own = together * feat
    count = together // 2 * (NLON // 4)
    steps = lats // together
    part = pltpu.VMEM((2, NLON // 2, own), jnp.float32)
    return pl.pallas_call(
        functools.partial(to_grid_kernel, steps),
        grid_spec=pltpu.PrefetchScalarGridSpec(
            num_scalar_prefetch=1,
            grid=(steps + 1,),
            in_specs=[
                WHOLE,
                pl.BlockSpec((depth, 2 * own), lambda i, s: (0, jnp.minimum(i, steps - 1))),
            ],
            out_specs=[
                pl.BlockSpec((NLON, own), lambda i, s: (0, jnp.maximum(i - 1, 0))),
                pl.BlockSpec((slot_total, feat), lambda i, s: (0, 0)),
            ],
            scratch_shapes=[
                pltpu.VMEM((count, feat), jnp.float32),
                pltpu.VMEM((slot_total, feat), jnp.float32),
                part,
                part,
            ],
        ),
        out_shape=[
            pltpu.HBM((NLON, lats * feat), jnp.bfloat16),
            jax.ShapeDtypeStruct((slot_total, feat), jnp.bfloat16),
        ],
        compiler_params=params(36),
        name="to_grid",
    )(slots, table, in_hbm(coeffs))


def silu(v):
    return 0.5 * v * (1.0 + jnp.tanh(0.5 * v))


def network_kernel(cols, weight_in, weight_mid, weight_out, out):
    parts = 2
    rows = out.shape[0] // parts

    def enter(part):
        hidden = jnp.dot(
            cols[part * rows : (part + 1) * rows],
            weight_in[...],
            preferred_element_type=jnp.float32,
        )
        return silu(hidden).astype(jnp.bfloat16)

    def leave(part, deeper):
        result = jnp.dot(deeper, weight_out[...], preferred_element_type=jnp.float32)
        out[part * rows : (part + 1) * rows] = result.astype(jnp.bfloat16)

    hidden, deeper = enter(0), None
    for part in range(parts):
        current = hidden
        if part + 1 < parts:
            hidden = enter(part + 1)
        middle = jnp.dot(current, weight_mid[...], preferred_element_type=jnp.float32)
        if deeper is not None:
            leave(part - 1, deeper)
        deeper = silu(middle).astype(jnp.bfloat16)
    leave(parts - 1, deeper)


def network(columns, weight_in, weight_mid, weight_out):
    rows, feat = columns.shape
    hid = weight_in.shape[1]
    block = rows // 4
    return pl.pallas_call(
        network_kernel,
        grid=(rows // block,),
        in_specs=[
            pl.BlockSpec((block, feat), lambda i: (i, 0)),
            WHOLE,
            WHOLE,
            WHOLE,
        ],
        out_specs=pl.BlockSpec((block, feat), lambda i: (i, 0)),
        out_shape=jax.ShapeDtypeStruct((rows, feat), jnp.bfloat16),
        compiler_params=params(36),
        name="network",
    )(columns, weight_in, weight_mid, weight_out)


def to_waves_kernel(steps, slots, table, forced, answers, out, wide, *held):
    step = pl.program_id(0)
    count, feat = held[1].shape
    lanes = forced.shape[1]
    half = table.shape[2]
    eighth = half // 4
    quarter = 2 * eighth

    def collect(number, cols, start, size):
        for k in range(start, start + size):
            cols[pl.ds(k, 1), :] = wide[pl.ds(slots[number * count + k], 1), :]

    def fold(number, slot):
        folded, cols, next_cols = slot
        after = jnp.minimum(number + 1, steps - 1)
        for i in range(count // quarter):
            coarse = cols[i * quarter : (i + 1) * quarter, :]
            before = pltpu.roll(coarse, 1, axis=0)
            following = pltpu.roll(coarse, quarter - 1, axis=0)
            for u in range(4):
                w, v, x = SPREAD[u]
                fine = v * coarse + (w * before if w else x * following)
                rows = slice(u * eighth, (u + 1) * eighth)
                far_rows = slice(half + u * eighth, half + (u + 1) * eighth)
                for t in (2 * i, 2 * i + 1):
                    own = slice(t * feat, (t + 1) * feat)
                    near = forced[rows, own] + fine[:eighth]
                    far = forced[far_rows, own] + fine[eighth:]
                    folded[0, rows, own] = (near + far).astype(jnp.bfloat16)
                    folded[1, rows, own] = (near - far).astype(jnp.bfloat16)
                if u % 2 == 1:
                    size = eighth
                    collect(after, next_cols, (2 * i + u // 2) * size, size)
                    yield

    def transform(_, slot):
        folded = slot[0]
        for parity in range(2):
            for at in range(0, lanes, 2 * feat):
                start = parity * lanes + at
                out[:, start : start + 2 * feat] = jnp.dot(
                    table[parity],
                    folded[parity, :, at : at + 2 * feat],
                    preferred_element_type=jnp.float32,
                ).astype(jnp.bfloat16)
                yield

    @pl.when(step == 0)
    def _():
        wide[...] = answers[...].astype(jnp.float32)
        collect(0, held[1], 0, count)

    staggered(
        step,
        steps,
        fold,
        transform,
        ((held[0], held[1], held[3]), (held[2], held[3], held[1])),
    )


def to_waves(slots, table, forced, answers):
    lanes = forced.shape[1]
    slot_total, feat = answers.shape
    depth = table.shape[1]
    lats = lanes // feat
    together = lats_together(lats)
    own = together * feat
    count = together // 2 * (NLON // 4)
    steps = lats // together
    slot = [
        pltpu.VMEM((2, NLON // 2, own), jnp.bfloat16),
        pltpu.VMEM((count, feat), jnp.float32),
    ]
    return pl.pallas_call(
        functools.partial(to_waves_kernel, steps),
        grid_spec=pltpu.PrefetchScalarGridSpec(
            num_scalar_prefetch=1,
            grid=(steps + 1,),
            in_specs=[
                WHOLE,
                pl.BlockSpec((NLON, own), lambda i, s: (0, jnp.minimum(i, steps - 1))),
                WHOLE,
            ],
            out_specs=pl.BlockSpec((depth, 2 * own), lambda i, s: (0, jnp.maximum(i - 1, 0))),
            scratch_shapes=[
                pltpu.VMEM((slot_total, feat), jnp.float32),
                *slot,
                *slot,
            ],
        ),
        out_shape=pltpu.HBM((depth, 2 * lanes), jnp.bfloat16),
        compiler_params=params(36),
        name="to_waves",
    )(slots, table, in_hbm(forced), answers)


def forward_legendre_kernel(steps, low, coeffs, leg, merge, out, *slots):
    step = pl.program_id(0)
    group, degrees, channels = out.shape
    feat = channels // 2
    lat_total = leg.shape[2]
    devices, rows = coeffs.shape[:2]
    lats = lat_total // devices
    pitch = lat_total + PITCH_EXTRA
    middle = (degrees - 1) // 2

    def turn(_, held):
        for d in range(devices):
            for a in range(lats):
                for parity in range(2):
                    start = parity * rows * pitch + d * lats + a
                    lane = lane_start(a, parity, lats, feat)
                    held[pl.ds(start, rows, stride=pitch), :] = coeffs[
                        d, :, lane : lane + feat
                    ].astype(jnp.float32)
            if (d + 1) % (devices // 4) == 0:
                yield

    first_pair = lax.axis_index("wave") * steps * group

    def transform(number, held):
        waiting = None
        for g in range(group):
            own_low = low[first_pair + number * group + g]
            lower = degrees - 1 - own_low
            sides = []
            for s in range(2):
                parity = (own_low + s) % 2
                parts = []
                for r in range(2):
                    start = (parity * rows + 2 * g + r) * pitch
                    parts.append(held[pl.ds(pl.multiple_of(start, 8), lat_total), :])
                sides.append(jnp.concatenate(parts, axis=1).astype(jnp.bfloat16))
            first = jnp.dot(leg[g], sides[0], preferred_element_type=jnp.float32)
            second = jnp.dot(leg[g, middle:], sides[1], preferred_element_type=jnp.float32)
            if waiting is not None:
                finish(g - 1, waiting)
            on_first = lax.broadcasted_iota(jnp.int32, second.shape, 0) < lower - middle
            chosen = jnp.concatenate(
                [first[:middle], jnp.where(on_first, first[middle:], second)], axis=0
            )
            waiting = chosen.astype(jnp.bfloat16)
            yield
        finish(group - 1, waiting)

    def finish(g, chosen):
        out[g] = jnp.dot(chosen, merge[...], preferred_element_type=jnp.float32).astype(
            jnp.bfloat16
        )

    staggered(step, steps, turn, transform, slots)


def forward_legendre(coeffs, legendre, pair_low, channels):
    devices, rows, lanes = coeffs.shape
    pairs, degrees, lat_total = legendre.shape
    group = group_of(pairs)
    steps = pairs // group
    slot = pltpu.VMEM(((4 * group + 1) * (lat_total + PITCH_EXTRA), channels // 2), jnp.float32)
    return pl.pallas_call(
        functools.partial(forward_legendre_kernel, steps),
        grid=(steps + 1,),
        in_specs=[
            pl.BlockSpec(memory_space=pltpu.SMEM),
            pl.BlockSpec(
                (devices, 2 * group, lanes), lambda i: (0, jnp.minimum(i, steps - 1), 0)
            ),
            pl.BlockSpec((group, degrees, lat_total), lambda i: (jnp.maximum(i - 1, 0), 0, 0)),
            pl.BlockSpec((channels, channels), lambda i: (0, 0)),
        ],
        out_specs=pl.BlockSpec((group, degrees, channels), lambda i: (jnp.maximum(i - 1, 0), 0, 0)),
        out_shape=jax.ShapeDtypeStruct((pairs, degrees, channels), jnp.bfloat16),
        scratch_shapes=[slot, slot],
        compiler_params=params(56),
        name="forward_legendre",
    )(pair_low, in_hbm(coeffs), in_hbm(legendre), split_matrix(channels).T)


def exchange(blocks):
    return lax.all_to_all(blocks, "wave", split_axis=0, concat_axis=0, tiled=True)


def on_device(spectral, legendre, pair_low, routes, w_in, w_mid, w_out):
    _, degrees, channels = spectral.shape
    feat = channels // 2
    devices = lax.axis_size("wave")
    sent = inverse_legendre(spectral, jnp.swapaxes(legendre, 1, 2), pair_low, devices)
    arrived = exchange(sent)
    inverse_table, forward_table = zonal_tables(pair_low, degrees - 1)
    regimes = routes[:, 0]
    capacity = 2 * regimes.shape[0] // devices
    slots = regimes * capacity + slot_positions(regimes, devices)

    forced, outgoing = to_grid(
        slots, inverse_table, arrived.reshape(-1, arrived.shape[2]), devices * capacity, feat
    )
    columns = exchange(outgoing.reshape(devices, capacity, feat))
    answers = network(columns.reshape(-1, feat), w_in[0], w_mid[0], w_out[0])
    incoming = exchange(answers.reshape(devices, capacity, feat)).reshape(-1, feat)
    waves = to_waves(slots, forward_table, forced, incoming)
    received = exchange(waves.reshape(arrived.shape))
    return forward_legendre(received, legendre, pair_low, channels)


def solution(mesh):
    placed = (
        P(("grp", "wave"), None, None),
        P("wave", None, None),
        P(),
        P(("grp", "wave"), None),
        P("wave", None, None),
        P("wave", None, None),
        P("wave", None, None),
    )
    return jax.shard_map(
        on_device,
        mesh=mesh,
        in_specs=placed,
        out_specs=P(("grp", "wave"), None, None),
        check_vma=False,
    )
```
